512 devices in a mesh: row: 128 (over y, z, core), col: 4 (over x).
Axes of the slice: x: 4, y: 4, z: 16, core: 2. Of those that a mesh axis runs over, the one named last changes fastest.
Arguments:
- edge: bfloat16 [32768, 1536], P('row', 'col'), may hold values from -6 to 6
- corner: bfloat16 [1536, 1536], P(None, 'col'), may hold values from -0.15625 to 0.15625
- tri_inv: bfloat16 [1536, 1536], P(None, 'col'), as said below
- vector: float32 [32768, 1536], P('row', 'col'), may hold values from -6 to 6
Outputs:
- next_vector: float32 [32768, 1536], P('row', 'col')
- coeffs: float32 [2], replicated
The draws below stay inside these ranges and needn't reach their ends.
Inputs may be any that keep to these rules, and one draw needn't show every extreme that they name: tri_inv is upper triangular; its diagonal lies between 1 and 2.
All inputs are finite; a program needn't handle non-finite values.
Results may differ from the reference program's by a relative error of at most 0.0075.
Values may be sent and summed in bfloat16 or wider, within the bound.
No kernel may reach another device: no remote copies, remote signals or barrier semaphores. Data moves between devices by JAX's collectives and lax.ppermute only.
A program may use at most 64 MiB of HBM per device.

```python
import jax
import jax.numpy as jnp

CHI = 1536
ROWS = 32768


def draw_tri_inv(key, part):
    key = jax.random.fold_in(key, 7)
    key_diag, key_off = jax.random.split(key)
    diag_vals = jax.random.uniform(key_diag, (CHI,), jnp.float32, 1.0, 2.0)
    off = jax.random.normal(key_off, (CHI, CHI), jnp.float32)
    off = off * (0.5 / CHI ** 0.5)
    rows_index = jnp.arange(CHI)[:, None]
    cols_index = jnp.arange(CHI)[None, :]
    matrix = jnp.where(rows_index < cols_index, off, 0.0)
    matrix = jnp.where(rows_index == cols_index, diag_vals[:, None], matrix)
    return matrix.astype(jnp.bfloat16)


def block_levels(stream_key, extent, cuts, smallest, largest):
    factor_of, own = 1.0, jax.random.fold_in(stream_key, 6)
    for position, shards_of in cuts:
        steps = jnp.exp(jax.random.uniform(jax.random.fold_in(own, position), (shards_of,), jnp.float32, smallest / len(cuts), largest / len(cuts)))
        factor_of = factor_of * jnp.repeat(steps, extent[position] // shards_of).reshape([-1 if axis == position else 1 for axis in range(len(extent))])
    return factor_of


def scatter_about(key, dims, width, most, shards=(), dtype=jnp.bfloat16):
    values = jax.random.normal(key, dims, jnp.float32) * width
    if len(shards) > 0:
        values = block_levels(key, dims, shards, -0.22, 0.18) * values
    return jnp.clip(values, min=-most, max=most).astype(dtype)


def setup_inputs(seed: int = 0) -> dict:
    keys = jax.random.split(jax.random.key(seed), 5)
    edge = scatter_about(keys[0], (ROWS, CHI), 1.0, 6.0, ((0, 128), (1, 4)))
    corner = scatter_about(keys[1], (CHI, CHI), CHI ** -0.5, 0.15625, ((1, 4),))
    tri_inv = draw_tri_inv(jax.random.fold_in(keys[4], 71), 0)
    vector = scatter_about(keys[3], (ROWS, CHI), 1.0, 6.0, ((0, 128), (1, 4)), jnp.float32)
    return {"edge": edge, "corner": corner, "tri_inv": tri_inv, "vector": vector}


def reference(edge, corner, tri_inv, vector):
    half = jnp.dot(edge, corner, preferred_element_type=jnp.float32).astype(jnp.bfloat16)
    proj = jnp.dot(half, tri_inv, preferred_element_type=jnp.float32).astype(jnp.bfloat16)
    vec_low = vector.astype(jnp.bfloat16)
    gram = jnp.dot(proj.T, vec_low, preferred_element_type=jnp.float32) / ROWS
    rows_index = jnp.arange(CHI)[:, None]
    cols_index = jnp.arange(CHI)[None, :]
    sym = jnp.where(rows_index >= cols_index, gram, gram.T).astype(jnp.bfloat16)
    corrected = (vector - jnp.dot(proj, sym, preferred_element_type=jnp.float32)).astype(jnp.bfloat16)
    dhalf = jnp.dot(corrected, tri_inv.T, preferred_element_type=jnp.float32).astype(jnp.bfloat16)
    dedge = jnp.dot(dhalf, corner.T, preferred_element_type=jnp.float32)
    image = vector - dedge
    along = jnp.mean(vector * image)
    resid = image - along * vector
    scale = jnp.sqrt(jnp.mean(resid * resid) + 1e-06)
    return (resid / scale, jnp.stack([along, scale]))
```

```python
import jax
import jax.numpy as jnp
from jax import lax
from jax.sharding import Mesh, PartitionSpec as P

BF16 = jnp.bfloat16
F32 = jnp.float32
ROW = ("y", "zh", "zl", "core")


def swap(pieces, axis):
    return lax.all_to_all(pieces, axis, split_axis=0, concat_axis=0, tiled=True)


def spread(block, axis):
    members = lax.axis_size(axis)
    return swap(jnp.broadcast_to(block[None], (members, *block.shape)), axis)


def total(pieces):
    return jnp.sum(pieces.astype(F32), axis=0)


def scatter_sum(block, axis):
    members = lax.axis_size(axis)
    pieces = block.reshape(members, block.shape[0] // members, block.shape[1])
    return total(swap(pieces, axis))


def join_rows(blocks, axis):
    stacked = spread(blocks, axis)
    members, count, rows, width = stacked.shape
    return stacked.transpose(1, 0, 2, 3).reshape(count, members * rows, width)


def whole_map(corner, tri_inv):
    bond, width = corner.shape
    blocks = bond // width
    half = bond // 2
    start = lax.axis_index("core") * half
    both = jnp.stack(
        [
            lax.dynamic_slice_in_dim(corner, start, half, 0),
            lax.dynamic_slice_in_dim(tri_inv, start, half, 0),
        ]
    )
    wide = spread(both, "x")
    corner_half = wide[:, 0]
    tri = spread(wide[:, 1], "core")
    tri = tri.transpose(1, 0, 2, 3).reshape(blocks, bond, width)
    corner_half = corner_half.transpose(1, 0, 2).reshape(half, bond)
    columns = [
        jnp.dot(
            corner_half[:, : (b + 1) * width],
            tri[b, : (b + 1) * width],
            preferred_element_type=F32,
        ).astype(BF16)
        for b in range(blocks)
    ]
    mine = jnp.concatenate(columns, axis=1)
    return spread(mine, "core").reshape(bond, bond)


def on_device(edge, corner, tri_inv, vector):
    bond, width = corner.shape
    blocks = bond // width
    place = lax.axis_index("x")
    row_devices = lax.axis_size(ROW)
    rows_total = vector.shape[0] * row_devices

    edge_wide = lax.all_gather(edge, "x", axis=1, tiled=True)
    vec_low = vector.astype(BF16)
    cross = lax.dot_general(
        vec_low, edge_wide, (((0,), (0,)), ((), ())), preferred_element_type=F32
    )
    for axis in ("core", "y", "zl"):
        cross = scatter_sum(cross.astype(BF16), axis)
    cross = total(spread(cross.astype(BF16), "zh")) / rows_total

    full_map = whole_map(corner, tri_inv)
    proj_wide = jnp.dot(edge_wide, full_map, preferred_element_type=F32).astype(BF16)

    gram_t = jnp.dot(cross.astype(BF16), full_map, preferred_element_type=F32)
    own = gram_t.astype(BF16).reshape(-1, blocks, width).transpose(1, 0, 2)
    other = swap(own, "x")
    block_id = lax.broadcasted_iota(jnp.int32, own.shape, 0)
    chosen = jnp.where(block_id < place, other, own)
    for axis in ("zl", "y", "core"):
        chosen = join_rows(chosen, axis)
    block_id = lax.broadcasted_iota(jnp.int32, chosen.shape, 0)
    first = lax.broadcasted_iota(jnp.int32, chosen.shape, 1)
    second = lax.broadcasted_iota(jnp.int32, chosen.shape, 2)
    diagonal = block_id == place
    zero = jnp.zeros_like(chosen)
    straight = jnp.where((block_id < place) | (diagonal & (first <= second)), chosen, zero)
    turned = jnp.where((block_id > place) | (diagonal & (first < second)), chosen, zero)
    product = jnp.dot(
        proj_wide, straight.reshape(bond, width), preferred_element_type=F32
    ) + jnp.einsum(
        "rbk,bjk->rj",
        proj_wide.reshape(-1, blocks, width),
        turned,
        preferred_element_type=F32,
    )
    corrected = (vector - product).astype(BF16)
    corrected_wide = lax.all_gather(corrected, "x", axis=1, tiled=True)
    map_rows = lax.dynamic_slice_in_dim(full_map, place * width, width, 0)
    dedge = lax.dot_general(
        corrected_wide, map_rows, (((1,), (1,)), ((), ())), preferred_element_type=F32
    )

    sums = jnp.stack(
        [jnp.sum(vector * vector), jnp.sum(vector * dedge), jnp.sum(dedge * dedge)]
    )
    for axis in ("core", "x", "y", "zl", "zh"):
        sums = lax.psum(sums, axis)
    count = float(rows_total * bond)
    along = (sums[0] - sums[1]) / count
    keep = 1.0 - along
    spread_sq = (keep * keep * sums[0] - 2.0 * keep * sums[1] + sums[2]) / count
    scale = jnp.sqrt(jnp.maximum(spread_sq, 0.0) + 1e-06)
    return ((keep * vector - dedge) / scale, jnp.stack([along, scale]))


def solution(mesh):
    fine = Mesh(mesh.devices.reshape(4, 4, -1, 2, mesh.shape["col"]), ROW + ("x",))
    in_specs = (P(ROW, "x"), P(None, "x"), P(None, "x"), P(ROW, "x"))
    out_specs = (P(ROW, "x"), P())
    return jax.shard_map(
        on_device, mesh=fine, in_specs=in_specs, out_specs=out_specs, check_vma=False
    )
```

```python
import jax
import jax.numpy as jnp
from jax import lax
from jax.sharding import Mesh, PartitionSpec as P

BF16 = jnp.bfloat16
F32 = jnp.float32
ROW = ("y", "zh", "zl", "core")


def swap(pieces, axis):
    return lax.all_to_all(pieces, axis, split_axis=0, concat_axis=0, tiled=True)


def spread(block, axis):
    members = lax.axis_size(axis)
    return swap(jnp.broadcast_to(block[None], (members, *block.shape)), axis)


def total(pieces):
    return jnp.sum(pieces.astype(F32), axis=0)


def scatter_sum(block, axis):
    members = lax.axis_size(axis)
    pieces = block.reshape(members, block.shape[0] // members, block.shape[1])
    return total(swap(pieces, axis))


def join_rows(blocks, axis):
    stacked = spread(blocks, axis)
    members, count, rows, width = stacked.shape
    return stacked.transpose(1, 0, 2, 3).reshape(count, members * rows, width)


def on_device(edge, corner, tri_inv, vector):
    bond, width = corner.shape
    blocks = bond // width
    place = lax.axis_index("x")
    row_devices = lax.axis_size(ROW)
    rows_total = vector.shape[0] * row_devices

    edge_wide = lax.all_gather(edge, "x", axis=1, tiled=True)
    edge_wide, corner = lax.optimization_barrier((edge_wide, corner))
    corner_wide = lax.all_gather(corner, "x", axis=1, tiled=True)
    vec_low = vector.astype(BF16)
    cross = lax.dot_general(
        vec_low, edge_wide, (((0,), (0,)), ((), ())), preferred_element_type=F32
    )
    for axis in ("core", "y", "zl"):
        cross = scatter_sum(cross.astype(BF16), axis)
    cross = total(spread(cross.astype(BF16), "zh")) / rows_total
    cross_all = spread(cross.astype(BF16), "x").reshape(-1, bond)

    own_map = jnp.dot(corner_wide, tri_inv, preferred_element_type=F32).astype(BF16)
    proj = jnp.dot(edge_wide, own_map, preferred_element_type=F32).astype(BF16)

    other = jnp.dot(cross_all, own_map, preferred_element_type=F32).astype(BF16)
    other = other.reshape(blocks, -1, width)
    own = swap(other, "x")
    block_id = lax.broadcasted_iota(jnp.int32, own.shape, 0)
    chosen = jnp.where(block_id < place, other, own)
    late = jnp.concatenate(
        [
            jnp.broadcast_to(proj[None], (blocks, *proj.shape)),
            own_map.reshape(blocks, width, width),
        ],
        axis=1,
    )
    late, chosen = lax.optimization_barrier((late, chosen))
    late = swap(late, "x")
    proj_blocks, map_blocks = late[:, : proj.shape[0]], late[:, proj.shape[0] :]
    for axis in ("zl", "y", "core"):
        chosen = join_rows(chosen, axis)
    block_id = lax.broadcasted_iota(jnp.int32, chosen.shape, 0)
    first = lax.broadcasted_iota(jnp.int32, chosen.shape, 1)
    second = lax.broadcasted_iota(jnp.int32, chosen.shape, 2)
    diagonal = block_id == place
    zero = jnp.zeros_like(chosen)
    straight = jnp.where((block_id < place) | (diagonal & (first <= second)), chosen, zero)
    turned = jnp.where((block_id > place) | (diagonal & (first < second)), chosen, zero)
    product = sum(
        jnp.dot(proj_blocks[k], straight[k], preferred_element_type=F32)
        + lax.dot_general(
            proj_blocks[k], turned[k], (((1,), (1,)), ((), ())), preferred_element_type=F32
        )
        for k in range(blocks)
    )
    corrected = (vector - product).astype(BF16)
    corrected_wide = lax.all_gather(corrected, "x", axis=1, tiled=True)
    dedge = sum(
        lax.dot_general(
            corrected_wide[:, k * width : (k + 1) * width],
            map_blocks[k],
            (((1,), (1,)), ((), ())),
            preferred_element_type=F32,
        )
        for k in range(blocks)
    )

    sums = jnp.stack(
        [jnp.sum(vector * vector), jnp.sum(vector * dedge), jnp.sum(dedge * dedge)]
    )
    for axis in ("core", "x", "y", "zl", "zh"):
        sums = lax.psum(sums, axis)
    count = float(rows_total * bond)
    along = (sums[0] - sums[1]) / count
    keep = 1.0 - along
    spread_sq = (keep * keep * sums[0] - 2.0 * keep * sums[1] + sums[2]) / count
    scale = jnp.sqrt(jnp.maximum(spread_sq, 0.0) + 1e-06)
    return ((keep * vector - dedge) / scale, jnp.stack([along, scale]))


def solution(mesh):
    fine = Mesh(mesh.devices.reshape(4, 4, -1, 2, mesh.shape["col"]), ROW + ("x",))
    in_specs = (P(ROW, "x"), P(None, "x"), P(None, "x"), P(ROW, "x"))
    out_specs = (P(ROW, "x"), P())
    return jax.shard_map(
        on_device, mesh=fine, in_specs=in_specs, out_specs=out_specs, check_vma=False
    )
```

```python
import functools

import jax
import jax.numpy as jnp
from jax import lax
from jax.experimental import pallas as pl
from jax.experimental.pallas import tpu as pltpu
from jax.sharding import Mesh, PartitionSpec as P

BF16 = jnp.bfloat16
F32 = jnp.float32
ROW = ("y", "zh", "zl", "core")
VMEM = pl.BlockSpec(memory_space=pltpu.VMEM)
SMEM = pl.BlockSpec(memory_space=pltpu.SMEM)
PARAMS = pltpu.CompilerParams(vmem_limit_bytes=48 * 1024 * 1024)


def swap(pieces, axis):
    return lax.all_to_all(pieces, axis, split_axis=0, concat_axis=0, tiled=True)


def spread(block, axis):
    members = lax.axis_size(axis)
    return swap(jnp.broadcast_to(block[None], (members, *block.shape)), axis)


def total(pieces):
    return jnp.sum(pieces.astype(F32), axis=0)


def scatter_sum(block, axis):
    members = lax.axis_size(axis)
    pieces = block.reshape(members, block.shape[0] // members, block.shape[1])
    return total(swap(pieces, axis))


def join_rows(blocks, axis):
    stacked = spread(blocks, axis)
    members, count, rows, width = stacked.shape
    return stacked.transpose(1, 0, 2, 3).reshape(count, members * rows, width)


def dot(a, b):
    return jnp.dot(a, b, preferred_element_type=F32)


def dot_turned(a, b):
    return lax.dot_general(a, b, (((1,), (1,)), ((), ())), preferred_element_type=F32)


def correct_kernel(place, vec, proj, *refs):
    *late, sym, out = refs
    rows = vec.shape[0]
    diag = sym[0]
    first = lax.broadcasted_iota(jnp.int32, diag.shape, 0)
    second = lax.broadcasted_iota(jnp.int32, diag.shape, 1)
    zero = jnp.zeros_like(diag)
    acc = dot(proj[...], jnp.where(first <= second, diag, zero))
    acc += dot_turned(proj[...], jnp.where(first < second, diag, zero))
    for s, piece in enumerate(late, 1):
        part = piece[:rows]
        straight = jnp.broadcast_to(s <= place[0], diag.shape)
        acc += dot(part, jnp.where(straight, sym[s], zero))
        acc += dot_turned(part, jnp.where(straight, zero, sym[s]))
    out[...] = (vec[...] - acc).astype(out.dtype)


def fold(values):
    line = jnp.sum(values, axis=0, keepdims=True)
    return sum(line[:, i : i + 128] for i in range(0, values.shape[1], 128))


def edge_kernel(place, vec, wide, own_rows, *refs):
    *late, dedge, sums = refs
    rows, width = vec.shape
    blocks = len(late) + 1
    acc = jnp.zeros((rows, width), F32)
    for s in range(blocks):
        k = lax.rem(place[0] + blocks - s, blocks)
        part = wide[:, pl.ds(pl.multiple_of(k * width, 128), width)]
        acc += dot_turned(part, own_rows[...] if s == 0 else late[s - 1][rows:])
    v = vec[...]
    dedge[...] = acc
    sums[...] = jnp.concatenate(
        [fold(v * v), fold(v * acc), fold(acc * acc), jnp.zeros((5, 128), F32)], axis=0
    )


def finish_kernel(count, sums, vec, dedge, out, coeffs):
    vv, vd, dd = (jnp.sum(sums[i : i + 1], axis=1, keepdims=True) for i in range(3))
    along = (vv - vd) / count
    keep = 1.0 - along
    square = (keep * keep * vv - 2.0 * keep * vd + dd) / count
    scale = jnp.sqrt(jnp.maximum(square, 0.0) + 1e-06)
    inverse = 1.0 / scale
    out[...] = (keep * vec[...] - dedge[...]) * inverse
    coeffs[0] = along[0, 0]
    coeffs[1] = scale[0, 0]


def on_device(edge, corner, tri_inv, vector):
    bond, width = corner.shape
    rows = vector.shape[0]
    blocks = bond // width
    place = lax.axis_index("x")
    here = place[None]
    rows_total = rows * lax.axis_size(ROW)

    edge_wide = lax.all_gather(edge, "x", axis=1, tiled=True)
    edge_wide, corner = lax.optimization_barrier((edge_wide, corner))
    corner_wide = lax.all_gather(corner, "x", axis=1, tiled=True)
    vec_low = vector.astype(BF16)
    cross = lax.dot_general(
        vec_low, edge_wide, (((0,), (0,)), ((), ())), preferred_element_type=F32
    )
    for axis in ("core", "y", "zl"):
        cross = scatter_sum(cross.astype(BF16), axis)
    cross = lax.psum(cross, "zh") / rows_total
    cross_all = spread(cross.astype(BF16), "x").reshape(-1, bond)

    other = dot(dot(cross_all, corner_wide).astype(BF16), tri_inv).astype(BF16)
    other = other.reshape(blocks, -1, width)
    own = swap(other, "x")

    own_map = dot(corner_wide, tri_inv).astype(BF16)
    proj = dot(edge_wide, own_map).astype(BF16)

    def block_of(s):
        k = lax.rem(place + blocks - s, blocks)
        source = own if s == 0 else jnp.where(s <= place, other, own)
        return lax.dynamic_index_in_dim(source, k, 0, keepdims=False)

    chosen = jnp.stack([block_of(s) for s in range(blocks)])

    def piece_for(s):
        k = lax.rem(place + s, blocks)
        return lax.dynamic_slice_in_dim(own_map, k * width, width, 0)

    pieces = [jnp.concatenate([proj, piece_for(s)]) for s in range(1, blocks)]
    pieces, chosen = lax.optimization_barrier((pieces, chosen))
    late = [
        lax.ppermute(piece, "x", [(i, (i + s) % blocks) for i in range(blocks)])
        for s, piece in enumerate(pieces, 1)
    ]
    for axis in ("zl", "y", "core"):
        chosen = join_rows(chosen, axis)

    corrected = pl.pallas_call(
        correct_kernel,
        out_shape=jax.ShapeDtypeStruct((rows, width), BF16),
        in_specs=[SMEM] + [VMEM] * (blocks + 2),
        out_specs=VMEM,
        compiler_params=PARAMS,
    )(here, vector, proj, *late, chosen)
    corrected_wide = lax.all_gather(corrected, "x", axis=1, tiled=True)
    dedge, sums = pl.pallas_call(
        edge_kernel,
        out_shape=(
            jax.ShapeDtypeStruct((rows, width), F32),
            jax.ShapeDtypeStruct((8, 128), F32),
        ),
        in_specs=[SMEM] + [VMEM] * (blocks + 2),
        out_specs=(VMEM, VMEM),
        compiler_params=PARAMS,
    )(here, vector, corrected_wide, piece_for(0), *late)
    for axis in ("core", "x", "y", "zl", "zh"):
        sums = lax.psum(sums, axis)
    return pl.pallas_call(
        functools.partial(finish_kernel, float(rows_total * bond)),
        out_shape=(
            jax.ShapeDtypeStruct((rows, width), F32),
            jax.ShapeDtypeStruct((2,), F32),
        ),
        in_specs=[VMEM] * 3,
        out_specs=(VMEM, SMEM),
        compiler_params=PARAMS,
    )(sums, vector, dedge)


def solution(mesh):
    fine = Mesh(mesh.devices.reshape(4, 4, -1, 2, mesh.shape["col"]), ROW + ("x",))
    in_specs = (P(ROW, "x"), P(None, "x"), P(None, "x"), P(ROW, "x"))
    out_specs = (P(ROW, "x"), P())
    return jax.shard_map(
        on_device, mesh=fine, in_specs=in_specs, out_specs=out_specs, check_vma=False
    )
```

```python
import functools

import jax
import jax.numpy as jnp
from jax import lax
from jax.experimental import pallas as pl
from jax.experimental.pallas import tpu as pltpu
from jax.sharding import Mesh, PartitionSpec as P

BF16 = jnp.bfloat16
F32 = jnp.float32
ROW = ("y", "zh", "zl", "core")
VMEM = pl.BlockSpec(memory_space=pltpu.VMEM)
SMEM = pl.BlockSpec(memory_space=pltpu.SMEM)
PARAMS = pltpu.CompilerParams(vmem_limit_bytes=48 * 1024 * 1024)


def swap(pieces, axis):
    return lax.all_to_all(pieces, axis, split_axis=0, concat_axis=0, tiled=True)


def spread(block, axis):
    members = lax.axis_size(axis)
    return swap(jnp.broadcast_to(block[None], (members, *block.shape)), axis)


def total(pieces):
    return jnp.sum(pieces.astype(F32), axis=0)


def scatter_sum(block, axis):
    members = lax.axis_size(axis)
    pieces = block.reshape(members, block.shape[0] // members, block.shape[1])
    return total(swap(pieces, axis))


def join_rows(blocks, axis):
    stacked = spread(blocks, axis)
    members, count, rows, width = stacked.shape
    return stacked.transpose(1, 0, 2, 3).reshape(count, members * rows, width)


def dot(a, b):
    return jnp.dot(a, b, preferred_element_type=F32)


def dot_turned(a, b):
    return lax.dot_general(a, b, (((1,), (1,)), ((), ())), preferred_element_type=F32)


def partial_kernel(place, vec, proj, sym, own_map, out):
    rows, width = vec.shape
    blocks = sym.shape[0]
    first = lax.broadcasted_iota(jnp.int32, (width, width), 0)
    second = lax.broadcasted_iota(jnp.int32, (width, width), 1)
    zero = jnp.zeros((width, width), BF16)
    acc = jnp.zeros((rows, width), F32)
    for k in range(blocks):
        shift = (place[0] - k) * width
        part = proj[k, :rows]
        acc += dot(part, jnp.where(first <= second + shift, sym[k], zero))
        acc += dot_turned(part, jnp.where(first < second - shift, sym[k], zero))
    corrected = (vec[...] - acc).astype(BF16)
    for k in range(blocks):
        share = dot_turned(corrected, own_map[k * width : (k + 1) * width])
        out[k] = share.astype(BF16)


def fold(values):
    line = jnp.sum(values, axis=0, keepdims=True)
    return sum(line[:, i : i + 128] for i in range(0, values.shape[1], 128))


def edge_kernel(vec, shares, dedge, sums):
    acc = sum(shares[k].astype(F32) for k in range(shares.shape[0]))
    v = vec[...]
    dedge[...] = acc
    sums[...] = jnp.concatenate(
        [fold(v * v), fold(v * acc), fold(acc * acc), jnp.zeros((5, 128), F32)], axis=0
    )


def finish_kernel(count, sums, vec, dedge, out, coeffs):
    vv, vd, dd = (jnp.sum(sums[i : i + 1], axis=1, keepdims=True) for i in range(3))
    along = (vv - vd) / count
    keep = 1.0 - along
    square = (keep * keep * vv - 2.0 * keep * vd + dd) / count
    scale = jnp.sqrt(jnp.maximum(square, 0.0) + 1e-06)
    inverse = 1.0 / scale
    out[...] = (keep * vec[...] - dedge[...]) * inverse
    coeffs[0] = along[0, 0]
    coeffs[1] = scale[0, 0]


def on_device(edge, corner, tri_inv, vector):
    bond, width = corner.shape
    rows = vector.shape[0]
    blocks = bond // width
    place = lax.axis_index("x")
    here = place[None]
    rows_total = rows * lax.axis_size(ROW)

    before = lax.broadcasted_iota(jnp.int32, (blocks, 1, 1), 0) < place
    edge, here, before = lax.optimization_barrier((edge, here, before))
    edge_wide = lax.all_gather(edge, "x", axis=1, tiled=True)
    edge_wide, corner = lax.optimization_barrier((edge_wide, corner))
    corner_wide = lax.all_gather(corner, "x", axis=1, tiled=True)
    vec_low = vector.astype(BF16)
    cross = lax.dot_general(
        vec_low, edge_wide, (((0,), (0,)), ((), ())), preferred_element_type=F32
    )
    cross = cross * (1.0 / rows_total)
    for axis in ("core", "y", "zl"):
        cross = scatter_sum(cross.astype(BF16), axis)
    cross = total(spread(cross.astype(BF16), "zh"))
    cross_all = spread(cross.astype(BF16), "x").reshape(-1, bond)

    other = dot(dot(cross_all, corner_wide).astype(BF16), tri_inv).astype(BF16)
    other = other.reshape(blocks, -1, width)
    own = swap(other, "x")

    own_map = dot(corner_wide, tri_inv).astype(BF16)
    proj = dot(edge_wide, own_map).astype(BF16)
    proj = jnp.concatenate([proj, own_map[: width - rows]])
    proj_blocks = lax.all_gather(proj, "x", axis=0)

    chosen = jnp.where(before, other, own)
    for axis in ("zl", "y", "core"):
        chosen = join_rows(chosen, axis)

    shares = pl.pallas_call(
        partial_kernel,
        out_shape=jax.ShapeDtypeStruct((blocks, rows, width), BF16),
        in_specs=[SMEM] + [VMEM] * 4,
        out_specs=VMEM,
        compiler_params=PARAMS,
    )(here, vector, proj_blocks, chosen, own_map)
    shares = swap(shares, "x")
    dedge, sums = pl.pallas_call(
        edge_kernel,
        out_shape=(
            jax.ShapeDtypeStruct((rows, width), F32),
            jax.ShapeDtypeStruct((8, 128), F32),
        ),
        in_specs=[VMEM, VMEM],
        out_specs=(VMEM, VMEM),
        compiler_params=PARAMS,
    )(vector, shares)
    for axis in ("core", "x", "y", "zl", "zh"):
        sums = lax.psum(sums, axis)
    return pl.pallas_call(
        functools.partial(finish_kernel, float(rows_total * bond)),
        out_shape=(
            jax.ShapeDtypeStruct((rows, width), F32),
            jax.ShapeDtypeStruct((2,), F32),
        ),
        in_specs=[VMEM] * 3,
        out_specs=(VMEM, SMEM),
        compiler_params=PARAMS,
    )(sums, vector, dedge)


def solution(mesh):
    fine = Mesh(mesh.devices.reshape(4, 4, -1, 2, mesh.shape["col"]), ROW + ("x",))
    in_specs = (P(ROW, "x"), P(None, "x"), P(None, "x"), P(ROW, "x"))
    out_specs = (P(ROW, "x"), P())
    return jax.shard_map(
        on_device, mesh=fine, in_specs=in_specs, out_specs=out_specs, check_vma=False
    )
```

```python
import functools

import jax
import jax.numpy as jnp
from jax import lax
from jax.experimental import pallas as pl
from jax.experimental.pallas import tpu as pltpu
from jax.sharding import Mesh, PartitionSpec as P

BF16 = jnp.bfloat16
F32 = jnp.float32
ROW = ("y", "zh", "zl", "core")
VMEM = pl.BlockSpec(memory_space=pltpu.VMEM)
SMEM = pl.BlockSpec(memory_space=pltpu.SMEM)
PARAMS = pltpu.CompilerParams(vmem_limit_bytes=48 * 1024 * 1024)


def swap(pieces, axis):
    return lax.all_to_all(pieces, axis, split_axis=0, concat_axis=0, tiled=True)


def spread(block, axis):
    members = lax.axis_size(axis)
    return swap(jnp.broadcast_to(block[None], (members, *block.shape)), axis)


def total(pieces):
    return jnp.sum(pieces.astype(F32), axis=0)


def scatter_sum(block, axis):
    members = lax.axis_size(axis)
    pieces = block.reshape(members, block.shape[0] // members, block.shape[1])
    return total(swap(pieces, axis))


def join_rows(blocks, axis):
    stacked = spread(blocks, axis)
    members, count, rows, width = stacked.shape
    return stacked.transpose(1, 0, 2, 3).reshape(count, members * rows, width)


def dot(a, b):
    return jnp.dot(a, b, preferred_element_type=F32)


def dot_turned(a, b):
    return lax.dot_general(a, b, (((1,), (1,)), ((), ())), preferred_element_type=F32)


def partial_kernel(place, vec, proj, sym, own_map, out):
    rows, width = vec.shape
    blocks = sym.shape[0]
    first = lax.broadcasted_iota(jnp.int32, (width, width), 0)
    second = lax.broadcasted_iota(jnp.int32, (width, width), 1)
    zero = jnp.zeros((width, width), BF16)
    acc = jnp.zeros((rows, width), F32)
    for k in range(blocks):
        shift = (place[0] - k) * width
        part = proj[k, :rows]
        acc += dot(part, jnp.where(first <= second + shift, sym[k], zero))
        acc += dot_turned(part, jnp.where(first < second - shift, sym[k], zero))
    corrected = (vec[...] - acc).astype(BF16)
    for k in range(blocks):
        share = dot_turned(corrected, own_map[k * width : (k + 1) * width])
        out[k] = share.astype(BF16)


def fold(values):
    line = jnp.sum(values, axis=0, keepdims=True)
    return sum(line[:, i : i + 128] for i in range(0, values.shape[1], 128))


def edge_kernel(vec, shares, dedge, sums):
    acc = sum(shares[k].astype(F32) for k in range(shares.shape[0]))
    v = vec[...]
    dedge[...] = acc
    sums[...] = jnp.concatenate(
        [fold(v * v), fold(v * acc), fold(acc * acc), jnp.zeros((5, 128), F32)], axis=0
    )


def finish_kernel(count, sums, vec, dedge, out, coeffs):
    vv, vd, dd = (jnp.sum(sums[i : i + 1], axis=1, keepdims=True) for i in range(3))
    along = (vv - vd) / count
    keep = 1.0 - along
    square = (keep * keep * vv - 2.0 * keep * vd + dd) / count
    scale = jnp.sqrt(jnp.maximum(square, 0.0) + 1e-06)
    inverse = 1.0 / scale
    out[...] = (keep * vec[...] - dedge[...]) * inverse
    coeffs[0] = along[0, 0]
    coeffs[1] = scale[0, 0]


def on_device(edge, corner, tri_inv, vector):
    bond, width = corner.shape
    rows = vector.shape[0]
    blocks = bond // width
    place = lax.axis_index("x")
    here = place[None]
    rows_total = rows * lax.axis_size(ROW)

    before = lax.broadcasted_iota(jnp.int32, (blocks, 1, 1), 0) < place
    edge, here, before = lax.optimization_barrier((edge, here, before))
    edge_wide = lax.all_gather(edge, "x", axis=1, tiled=True)
    half = bond // 2
    core = lax.axis_index("core")
    corner_rows = lax.dynamic_slice_in_dim(corner, core * half, half, 0)
    edge_wide, corner_rows = lax.optimization_barrier((edge_wide, corner_rows))
    corner_wide = lax.all_gather(corner_rows, "x", axis=1, tiled=True)
    vec_low = vector.astype(BF16)
    cross = lax.dot_general(
        vec_low, edge_wide, (((0,), (0,)), ((), ())), preferred_element_type=F32
    )
    cross = cross * (1.0 / rows_total)
    for axis in ("core", "y", "zl"):
        cross = scatter_sum(cross.astype(BF16), axis)
    cross = total(spread(cross.astype(BF16), "zh"))
    cross_all = spread(cross.astype(BF16), "x").reshape(-1, bond)

    mine = dot(corner_wide, tri_inv).astype(BF16)
    theirs = lax.ppermute(mine, "core", [(0, 1), (1, 0)])
    own_map = jnp.concatenate(
        [jnp.where(core == 0, mine, theirs), jnp.where(core == 0, theirs, mine)]
    )
    proj = dot(edge_wide, own_map).astype(BF16)

    other = dot(cross_all, own_map).astype(BF16).reshape(blocks, -1, width)
    own = swap(other, "x")

    proj = jnp.concatenate([proj, own_map[: width - rows]])
    proj_blocks = lax.all_gather(proj, "x", axis=0)

    chosen = jnp.where(before, other, own)
    for axis in ("zl", "y", "core"):
        chosen = join_rows(chosen, axis)

    shares = pl.pallas_call(
        partial_kernel,
        out_shape=jax.ShapeDtypeStruct((blocks, rows, width), BF16),
        in_specs=[SMEM] + [VMEM] * 4,
        out_specs=VMEM,
        compiler_params=PARAMS,
    )(here, vector, proj_blocks, chosen, own_map)
    shares = swap(shares, "x")
    dedge, sums = pl.pallas_call(
        edge_kernel,
        out_shape=(
            jax.ShapeDtypeStruct((rows, width), F32),
            jax.ShapeDtypeStruct((8, 128), F32),
        ),
        in_specs=[VMEM, VMEM],
        out_specs=(VMEM, VMEM),
        compiler_params=PARAMS,
    )(vector, shares)
    for axis in ("core", "x", "y", "zl", "zh"):
        sums = lax.psum(sums, axis)
    return pl.pallas_call(
        functools.partial(finish_kernel, float(rows_total * bond)),
        out_shape=(
            jax.ShapeDtypeStruct((rows, width), F32),
            jax.ShapeDtypeStruct((2,), F32),
        ),
        in_specs=[VMEM] * 3,
        out_specs=(VMEM, SMEM),
        compiler_params=PARAMS,
    )(sums, vector, dedge)


def solution(mesh):
    fine = Mesh(mesh.devices.reshape(4, 4, -1, 2, mesh.shape["col"]), ROW + ("x",))
    in_specs = (P(ROW, "x"), P(None, "x"), P(None, "x"), P(ROW, "x"))
    out_specs = (P(ROW, "x"), P())
    return jax.shard_map(
        on_device, mesh=fine, in_specs=in_specs, out_specs=out_specs, check_vma=False
    )
```

```python
import functools

import jax
import jax.numpy as jnp
from jax import lax
from jax.experimental import pallas as pl
from jax.experimental.pallas import tpu as pltpu
from jax.sharding import Mesh, PartitionSpec as P

BF16 = jnp.bfloat16
F32 = jnp.float32
ROW = ("y", "zh", "zl", "core")
VMEM = pl.BlockSpec(memory_space=pltpu.VMEM)
SMEM = pl.BlockSpec(memory_space=pltpu.SMEM)
PARAMS = pltpu.CompilerParams(vmem_limit_bytes=48 * 1024 * 1024)


def swap(pieces, axis):
    return lax.all_to_all(pieces, axis, split_axis=0, concat_axis=0, tiled=True)


def spread(block, axis):
    members = lax.axis_size(axis)
    return swap(jnp.broadcast_to(block[None], (members, *block.shape)), axis)


def total(pieces):
    return jnp.sum(pieces.astype(F32), axis=0)


def scatter_sum(block, axis):
    members = lax.axis_size(axis)
    pieces = block.reshape(members, block.shape[0] // members, block.shape[1])
    return total(swap(pieces, axis))


def join_rows(blocks, axis):
    stacked = spread(blocks, axis)
    members, count, rows, width = stacked.shape
    return stacked.transpose(1, 0, 2, 3).reshape(count, members * rows, width)


def dot(a, b):
    return jnp.dot(a, b, preferred_element_type=F32)


def dot_turned(a, b):
    return lax.dot_general(a, b, (((1,), (1,)), ((), ())), preferred_element_type=F32)


def map_half_kernel(after, corner_rows, tri_inv, out):
    del after
    out[...] = dot(corner_rows[...], tri_inv[...]).astype(BF16)


def join_kernel(core, mine, theirs, edge_wide, own_map, proj):
    half = mine.shape[0]
    rows = edge_wide.shape[0]
    low = jnp.broadcast_to(core[0] == 0, mine.shape)
    own_map[:half] = jnp.where(low, mine[...], theirs[...])
    own_map[half:] = jnp.where(low, theirs[...], mine[...])
    proj[:rows] = dot(edge_wide[...], own_map[...]).astype(BF16)
    proj[rows:] = jnp.zeros((proj.shape[0] - rows, proj.shape[1]), BF16)


def partial_kernel(place, vec, sym, proj_in, map_in, out, proj, own_map, sem):
    rows, width = vec.shape
    blocks = proj.shape[0]
    fetch_proj = pltpu.make_async_copy(proj_in.at[:, :rows], proj, sem.at[0])
    fetch_map = pltpu.make_async_copy(map_in, own_map, sem.at[1])
    fetch_proj.start()
    fetch_map.start()
    first = lax.broadcasted_iota(jnp.int32, (width, width), 0)
    second = lax.broadcasted_iota(jnp.int32, (width, width), 1)
    zero = jnp.zeros((width, width), BF16)
    acc = jnp.zeros((rows, width), F32)
    fetch_proj.wait()
    for k in range(blocks):
        shift = (place[0] - k) * width
        block = jnp.concatenate(
            [sym[c, y, k] for c in range(sym.shape[0]) for y in range(sym.shape[1])]
        )
        part = proj[k]
        acc += dot(part, jnp.where(first <= second + shift, block, zero))
        acc += dot_turned(part, jnp.where(first < second - shift, block, zero))
    corrected = (vec[...] - acc).astype(BF16)
    fetch_map.wait()
    for k in range(blocks):
        share = dot_turned(corrected, own_map[k * width : (k + 1) * width])
        out[k] = share.astype(BF16)


def fold(values):
    line = jnp.sum(values, axis=0, keepdims=True)
    return sum(line[:, i : i + 128] for i in range(0, values.shape[1], 128))


def edge_kernel(vec, shares, dedge, sums):
    acc = sum(shares[k].astype(F32) for k in range(shares.shape[0]))
    v = vec[...]
    dedge[...] = acc
    sums[...] = jnp.concatenate(
        [fold(v * v), fold(v * acc), fold(acc * acc), jnp.zeros((5, 128), F32)], axis=0
    )


def finish_kernel(count, sums, vec, dedge, out, coeffs):
    lines = sum(sums[i] for i in range(sums.shape[0]))
    vv, vd, dd = (jnp.sum(lines[i : i + 1], axis=1, keepdims=True) for i in range(3))
    along = (vv - vd) / count
    keep = 1.0 - along
    square = (keep * keep * vv - 2.0 * keep * vd + dd) / count
    scale = jnp.sqrt(jnp.maximum(square, 0.0) + 1e-06)
    inverse = 1.0 / scale
    out[...] = (keep * vec[...] - dedge[...]) * inverse
    coeffs[0] = along[0, 0]
    coeffs[1] = scale[0, 0]


def on_device(edge, corner, tri_inv, vector):
    bond, width = corner.shape
    rows = vector.shape[0]
    blocks = bond // width
    place = lax.axis_index("x")
    here = place[None]
    rows_total = rows * lax.axis_size(ROW)

    before = lax.broadcasted_iota(jnp.int32, (blocks, 1, 1), 0) < place
    core = lax.axis_index("core")
    core_here = core[None]
    edge, here, core_here, before = lax.optimization_barrier(
        (edge, here, core_here, before)
    )
    edge_wide = lax.all_gather(edge, "x", axis=1, tiled=True)
    half = bond // 2
    corner_rows = lax.dynamic_slice_in_dim(corner, core * half, half, 0)
    edge_wide, corner_rows = lax.optimization_barrier((edge_wide, corner_rows))
    corner_wide = lax.all_gather(corner_rows, "x", axis=1, tiled=True)
    vec_low = vector.astype(BF16)
    cross = lax.dot_general(
        vec_low, edge_wide, (((0,), (0,)), ((), ())), preferred_element_type=F32
    )
    cross = cross * (1.0 / rows_total)
    for axis in ("core", "y", "zl"):
        cross = scatter_sum(cross.astype(BF16), axis)
    cross = cross.astype(BF16)

    mine = pl.pallas_call(
        map_half_kernel,
        out_shape=jax.ShapeDtypeStruct((half, width), BF16),
        in_specs=[pl.BlockSpec(memory_space=pl.ANY), VMEM, VMEM],
        out_specs=VMEM,
        compiler_params=PARAMS,
        cost_estimate=pl.CostEstimate(
            flops=2 * half * bond * width, bytes_accessed=4 * half * bond, transcendentals=0
        ),
    )(cross, corner_wide, tri_inv)
    theirs = lax.ppermute(mine, "core", [(0, 1), (1, 0)])
    own_map, proj = pl.pallas_call(
        join_kernel,
        out_shape=(
            jax.ShapeDtypeStruct((bond, width), BF16),
            jax.ShapeDtypeStruct((width, width), BF16),
        ),
        in_specs=[SMEM] + [VMEM] * 3,
        out_specs=(VMEM, VMEM),
        compiler_params=PARAMS,
        cost_estimate=pl.CostEstimate(
            flops=2 * rows * bond * width, bytes_accessed=4 * half * bond, transcendentals=0
        ),
    )(core_here, mine, theirs, edge_wide)
    proj_blocks = lax.all_gather(proj, "x", axis=0)

    cross = total(spread(cross, "zh"))
    cross_all = spread(cross.astype(BF16), "x").reshape(-1, bond)
    other = dot(cross_all, own_map).astype(BF16).reshape(blocks, -1, width)
    own = swap(other, "x")
    chosen = join_rows(jnp.where(before, other, own), "zl")
    chosen = spread(spread(chosen, "y"), "core")

    shares = pl.pallas_call(
        partial_kernel,
        out_shape=jax.ShapeDtypeStruct((blocks, rows, width), BF16),
        in_specs=[SMEM, VMEM, VMEM] + [pl.BlockSpec(memory_space=pl.ANY)] * 2,
        out_specs=VMEM,
        scratch_shapes=[
            pltpu.VMEM((blocks, rows, width), BF16),
            pltpu.VMEM((bond, width), BF16),
            pltpu.SemaphoreType.DMA((2,)),
        ],
        compiler_params=PARAMS,
    )(here, vector, chosen, proj_blocks, own_map)
    shares = swap(shares, "x")
    dedge, sums = pl.pallas_call(
        edge_kernel,
        out_shape=(
            jax.ShapeDtypeStruct((rows, width), F32),
            jax.ShapeDtypeStruct((8, 128), F32),
        ),
        in_specs=[VMEM, VMEM],
        out_specs=(VMEM, VMEM),
        compiler_params=PARAMS,
    )(vector, shares)
    for axis in ("core", "x", "y", "zl"):
        sums = lax.psum(sums, axis)
    sums = spread(sums, "zh")
    return pl.pallas_call(
        functools.partial(finish_kernel, float(rows_total * bond)),
        out_shape=(
            jax.ShapeDtypeStruct((rows, width), F32),
            jax.ShapeDtypeStruct((2,), F32),
        ),
        in_specs=[VMEM] * 3,
        out_specs=(VMEM, SMEM),
        compiler_params=PARAMS,
    )(sums, vector, dedge)


def solution(mesh):
    fine = Mesh(mesh.devices.reshape(4, 4, -1, 2, mesh.shape["col"]), ROW + ("x",))
    in_specs = (P(ROW, "x"), P(None, "x"), P(None, "x"), P(ROW, "x"))
    out_specs = (P(ROW, "x"), P())
    return jax.shard_map(
        on_device, mesh=fine, in_specs=in_specs, out_specs=out_specs, check_vma=False
    )
```

```python
import functools

import jax
import jax.numpy as jnp
from jax import lax
from jax.experimental import pallas as pl
from jax.experimental.pallas import tpu as pltpu
from jax.sharding import Mesh, PartitionSpec as P

BF16 = jnp.bfloat16
F32 = jnp.float32
ROW = ("y", "zh", "zl", "core")
VMEM = pl.BlockSpec(memory_space=pltpu.VMEM)
SMEM = pl.BlockSpec(memory_space=pltpu.SMEM)
PARAMS = pltpu.CompilerParams(vmem_limit_bytes=14 * 1024 * 1024)
LARGE = pltpu.CompilerParams(vmem_limit_bytes=56 * 1024 * 1024)


def swap(pieces, axis):
    return lax.all_to_all(pieces, axis, split_axis=0, concat_axis=0, tiled=True)


def spread(block, axis):
    members = lax.axis_size(axis)
    return swap(jnp.broadcast_to(block[None], (members, *block.shape)), axis)


def total(pieces):
    return jnp.sum(pieces.astype(F32), axis=0)


def scatter_sum(block, axis):
    members = lax.axis_size(axis)
    pieces = block.reshape(members, block.shape[0] // members, block.shape[1])
    return total(swap(pieces, axis))


def join_rows(blocks, axis):
    stacked = spread(blocks, axis)
    members, count, rows, width = stacked.shape
    return stacked.transpose(1, 0, 2, 3).reshape(count, members * rows, width)


def dot(a, b):
    return jnp.dot(a, b, preferred_element_type=F32)


def dot_turned(a, b):
    return lax.dot_general(a, b, (((1,), (1,)), ((), ())), preferred_element_type=F32)


def map_kernel(corner_rows, tri_inv, edge_cols, slice_cols, own_map, proj, gram, acc, low):
    step = pl.program_id(0)
    rows = edge_cols.shape[0]
    own_map[...] = dot(corner_rows[...], tri_inv[...]).astype(BF16)

    @pl.when(step == 0)
    def _():
        acc[...] = jnp.zeros_like(acc)
        low[...] = jnp.zeros_like(low)
        proj[rows:] = jnp.zeros((proj.shape[0] - rows, proj.shape[1]), BF16)

    acc[...] += dot(edge_cols[...], own_map[...])
    low[...] += dot(slice_cols[...], own_map[...])

    @pl.when(step == pl.num_programs(0) - 1)
    def _():
        proj[:rows] = acc[...].astype(BF16)
        gram[...] = low[...].astype(BF16)


def partial_kernel(
    place, vec_in, sym_in, proj_in, map_in, out, vec, sym, proj, own_map, sem
):
    rows, width = vec.shape
    blocks = proj.shape[0]
    fetch_proj = pltpu.make_async_copy(proj_in.at[:, :rows], proj, sem.at[0])
    fetch_sym = pltpu.make_async_copy(sym_in, sym, sem.at[1])
    fetch_vec = pltpu.make_async_copy(vec_in, vec, sem.at[2])
    fetch_map = pltpu.make_async_copy(map_in, own_map, sem.at[3])
    for fetch in (fetch_proj, fetch_sym, fetch_vec, fetch_map):
        fetch.start()
    first = lax.broadcasted_iota(jnp.int32, (width, width), 0)
    second = lax.broadcasted_iota(jnp.int32, (width, width), 1)
    zero = jnp.zeros((width, width), BF16)
    acc = jnp.zeros((rows, width), F32)
    fetch_proj.wait()
    fetch_sym.wait()
    for k in range(blocks):
        shift = (place[0] - k) * width
        block = jnp.concatenate(
            [sym[c, y, k] for c in range(sym.shape[0]) for y in range(sym.shape[1])]
        )
        part = proj[k]
        acc += dot(part, jnp.where(first <= second + shift, block, zero))
        acc += dot_turned(part, jnp.where(first < second - shift, block, zero))
    fetch_vec.wait()
    corrected = (vec[...] - acc).astype(BF16)
    fetch_map.wait()
    for k in range(blocks):
        share = dot_turned(corrected, own_map[k * width : (k + 1) * width])
        out[k] = share.astype(BF16)


def fold(values):
    line = jnp.sum(values, axis=0, keepdims=True)
    return sum(line[:, i : i + 128] for i in range(0, values.shape[1], 128))


def edge_kernel(vec, shares, dedge, sums):
    acc = sum(shares[k].astype(F32) for k in range(shares.shape[0]))
    v = vec[...]
    dedge[...] = acc
    sums[...] = jnp.concatenate(
        [fold(v * v), fold(v * acc), fold(acc * acc), jnp.zeros((5, 128), F32)], axis=0
    )


def finish_kernel(count, sums, vec, dedge, out, coeffs):
    lines = sum(sums[i] for i in range(sums.shape[0]))
    vv, vd, dd = (jnp.sum(lines[i : i + 1], axis=1, keepdims=True) for i in range(3))
    along = (vv - vd) / count
    keep = 1.0 - along
    square = (keep * keep * vv - 2.0 * keep * vd + dd) / count
    scale = jnp.sqrt(jnp.maximum(square, 0.0) + 1e-06)
    inverse = 1.0 / scale
    out[...] = (keep * vec[...] - dedge[...]) * inverse
    coeffs[0] = along[0, 0]
    coeffs[1] = scale[0, 0]


def on_device(edge, corner, tri_inv, vector):
    bond, width = corner.shape
    rows = vector.shape[0]
    blocks = bond // width
    place = lax.axis_index("x")
    here = place[None]
    rows_total = rows * lax.axis_size(ROW)

    before = lax.broadcasted_iota(jnp.int32, (blocks, 1, 1), 0) < place
    edge, here, before = lax.optimization_barrier((edge, here, before))
    corner_wide = lax.all_gather(corner, "x", axis=1, tiled=True)
    edge_wide = lax.all_gather(edge, "x", axis=1, tiled=True)
    vec_low = vector.astype(BF16)
    cross = lax.dot_general(
        vec_low, edge_wide, (((0,), (0,)), ((), ())), preferred_element_type=F32
    )
    cross = cross * (1.0 / rows_total)
    for axis in ("core", "y", "zl"):
        cross = scatter_sum(cross.astype(BF16), axis)
    cross = total(spread(cross.astype(BF16), "zh")).astype(BF16)
    cross_all = spread(cross, "x").reshape(-1, bond)

    step = bond // 6
    own_map, proj, other = pl.pallas_call(
        map_kernel,
        grid=(bond // step,),
        out_shape=(
            jax.ShapeDtypeStruct((bond, width), BF16),
            jax.ShapeDtypeStruct((width, width), BF16),
            jax.ShapeDtypeStruct((cross_all.shape[0], width), BF16),
        ),
        in_specs=[
            pl.BlockSpec((step, bond), lambda i: (i, 0)),
            pl.BlockSpec((bond, width), lambda i: (0, 0)),
            pl.BlockSpec((rows, step), lambda i: (0, i)),
            pl.BlockSpec((cross_all.shape[0], step), lambda i: (0, i)),
        ],
        out_specs=(
            pl.BlockSpec((step, width), lambda i: (i, 0)),
            pl.BlockSpec((width, width), lambda i: (0, 0)),
            pl.BlockSpec((cross_all.shape[0], width), lambda i: (0, 0)),
        ),
        scratch_shapes=[
            pltpu.VMEM((rows, width), F32),
            pltpu.VMEM((cross_all.shape[0], width), F32),
        ],
        compiler_params=LARGE,
        cost_estimate=pl.CostEstimate(
            flops=2 * (bond + rows) * bond * width,
            bytes_accessed=2 * bond * (bond + 2 * width),
            transcendentals=0,
        ),
    )(corner_wide, tri_inv, edge_wide, cross_all)
    proj_blocks = lax.all_gather(proj, "x", axis=0)

    other = other.reshape(blocks, -1, width)
    own = swap(other, "x")
    chosen = join_rows(jnp.where(before, other, own), "zl")
    chosen = spread(spread(chosen, "y"), "core")

    shares = pl.pallas_call(
        partial_kernel,
        out_shape=jax.ShapeDtypeStruct((blocks, rows, width), BF16),
        in_specs=[SMEM] + [pl.BlockSpec(memory_space=pl.ANY)] * 4,
        out_specs=VMEM,
        scratch_shapes=[
            pltpu.VMEM((rows, width), F32),
            pltpu.VMEM(chosen.shape, BF16),
            pltpu.VMEM((blocks, rows, width), BF16),
            pltpu.VMEM((bond, width), BF16),
            pltpu.SemaphoreType.DMA((4,)),
        ],
        compiler_params=LARGE,
    )(here, vector, chosen, proj_blocks, own_map)
    shares = swap(shares, "x")
    dedge, sums = pl.pallas_call(
        edge_kernel,
        out_shape=(
            jax.ShapeDtypeStruct((rows, width), F32),
            jax.ShapeDtypeStruct((8, 128), F32),
        ),
        in_specs=[VMEM, VMEM],
        out_specs=(VMEM, VMEM),
        compiler_params=PARAMS,
    )(vector, shares)
    for axis in ("core", "x", "y", "zl"):
        sums = lax.psum(sums, axis)
    sums = spread(sums, "zh")
    return pl.pallas_call(
        functools.partial(finish_kernel, float(rows_total * bond)),
        out_shape=(
            jax.ShapeDtypeStruct((rows, width), F32),
            jax.ShapeDtypeStruct((2,), F32),
        ),
        in_specs=[VMEM] * 3,
        out_specs=(VMEM, SMEM),
        compiler_params=PARAMS,
    )(sums, vector, dedge)


def solution(mesh):
    fine = Mesh(mesh.devices.reshape(4, 4, -1, 2, mesh.shape["col"]), ROW + ("x",))
    in_specs = (P(ROW, "x"), P(None, "x"), P(None, "x"), P(ROW, "x"))
    out_specs = (P(ROW, "x"), P())
    return jax.shard_map(
        on_device, mesh=fine, in_specs=in_specs, out_specs=out_specs, check_vma=False
    )
```

```python
import functools

import jax
import jax.numpy as jnp
from jax import lax
from jax.experimental import pallas as pl
from jax.experimental.pallas import tpu as pltpu
from jax.sharding import Mesh, PartitionSpec as P

BF16 = jnp.bfloat16
F32 = jnp.float32
ROW = ("y", "zh", "zl", "core")
VMEM = pl.BlockSpec(memory_space=pltpu.VMEM)
SMEM = pl.BlockSpec(memory_space=pltpu.SMEM)
PARAMS = pltpu.CompilerParams(vmem_limit_bytes=10 * 1024 * 1024)


def swap(pieces, axis):
    return lax.all_to_all(pieces, axis, split_axis=0, concat_axis=0, tiled=True)


def spread(block, axis):
    members = lax.axis_size(axis)
    return swap(jnp.broadcast_to(block[None], (members, *block.shape)), axis)


def total(pieces):
    return jnp.sum(pieces.astype(F32), axis=0)


def scatter_sum(block, axis):
    members = lax.axis_size(axis)
    pieces = block.reshape(members, block.shape[0] // members, block.shape[1])
    return total(swap(pieces, axis))


def join_rows(blocks, axis):
    stacked = spread(blocks, axis)
    members, count, rows, width = stacked.shape
    return stacked.transpose(1, 0, 2, 3).reshape(count, members * rows, width)


def dot(a, b):
    return jnp.dot(a, b, preferred_element_type=F32)


def dot_turned(a, b):
    return lax.dot_general(a, b, (((1,), (1,)), ((), ())), preferred_element_type=F32)


def map_kernel(corner, tri_inv, edge, slices, own_map, proj, gram):
    bond = corner.shape[0]
    rows = edge.shape[0]
    step = bond // 6

    @pl.loop(0, bond, step=step)
    def _(i):
        part = pl.ds(pl.multiple_of(i, step), step)
        own_map[part] = dot(corner[part], tri_inv[...]).astype(BF16)

    proj[:rows] = dot(edge[...], own_map[...]).astype(BF16)
    proj[rows:] = jnp.zeros((proj.shape[0] - rows, proj.shape[1]), BF16)
    gram[...] = dot(slices[...], own_map[...]).astype(BF16)


def partial_kernel(place, vec, sym, proj, own_map, out):
    rows, width = vec.shape
    blocks = proj.shape[0]
    first = lax.broadcasted_iota(jnp.int32, (width, width), 0)
    second = lax.broadcasted_iota(jnp.int32, (width, width), 1)
    zero = jnp.zeros((width, width), BF16)
    acc = jnp.zeros((rows, width), F32)
    for k in range(blocks):
        shift = (place[0] - k) * width
        block = jnp.concatenate(
            [sym[c, y, k] for c in range(sym.shape[0]) for y in range(sym.shape[1])]
        )
        part = proj[k, :rows]
        acc += dot(part, jnp.where(first <= second + shift, block, zero))
        acc += dot_turned(part, jnp.where(first < second - shift, block, zero))
    corrected = (vec[...] - acc).astype(BF16)
    for k in range(blocks):
        share = dot_turned(corrected, own_map[k * width : (k + 1) * width])
        out[k] = share.astype(BF16)


def fold(values):
    line = jnp.sum(values, axis=0, keepdims=True)
    return sum(line[:, i : i + 128] for i in range(0, values.shape[1], 128))


def edge_kernel(vec, shares, dedge, sums):
    acc = sum(shares[k].astype(F32) for k in range(shares.shape[0]))
    v = vec[...]
    dedge[...] = acc
    sums[...] = jnp.concatenate(
        [fold(v * v), fold(v * acc), fold(acc * acc), jnp.zeros((5, 128), F32)], axis=0
    )


def finish_kernel(count, sums, vec, dedge, out, coeffs):
    lines = sum(sums[i] for i in range(sums.shape[0]))
    vv, vd, dd = (jnp.sum(lines[i : i + 1], axis=1, keepdims=True) for i in range(3))
    along = (vv - vd) / count
    keep = 1.0 - along
    square = (keep * keep * vv - 2.0 * keep * vd + dd) / count
    scale = jnp.sqrt(jnp.maximum(square, 0.0) + 1e-06)
    inverse = 1.0 / scale
    out[...] = (keep * vec[...] - dedge[...]) * inverse
    coeffs[0] = along[0, 0]
    coeffs[1] = scale[0, 0]


def on_device(edge, corner, tri_inv, vector):
    bond, width = corner.shape
    rows = vector.shape[0]
    blocks = bond // width
    place = lax.axis_index("x")
    here = place[None]
    rows_total = rows * lax.axis_size(ROW)

    before = lax.broadcasted_iota(jnp.int32, (blocks, 1, 1), 0) < place
    edge, here, before = lax.optimization_barrier((edge, here, before))
    corner_wide = lax.all_gather(corner, "x", axis=1, tiled=True)
    edge_wide = lax.all_gather(edge, "x", axis=1, tiled=True)
    vec_low = vector.astype(BF16)
    cross = lax.dot_general(
        vec_low, edge_wide, (((0,), (0,)), ((), ())), preferred_element_type=F32
    )
    cross = cross * (1.0 / rows_total)
    for axis in ("core", "y", "zl"):
        cross = scatter_sum(cross.astype(BF16), axis)
    cross = total(spread(cross.astype(BF16), "zh")).astype(BF16)
    cross, corner_wide = lax.optimization_barrier((cross, corner_wide))
    cross_all = spread(cross, "x").reshape(-1, bond)

    own_map, proj, other = pl.pallas_call(
        map_kernel,
        out_shape=(
            jax.ShapeDtypeStruct((bond, width), BF16),
            jax.ShapeDtypeStruct((width, width), BF16),
            jax.ShapeDtypeStruct((cross_all.shape[0], width), BF16),
        ),
        in_specs=[VMEM] * 4,
        out_specs=(VMEM,) * 3,
        compiler_params=PARAMS,
        cost_estimate=pl.CostEstimate(
            flops=2 * (bond + rows) * bond * width,
            bytes_accessed=2 * bond * (bond + 2 * width),
            transcendentals=0,
        ),
    )(corner_wide, tri_inv, edge_wide, cross_all)
    proj_blocks = lax.all_gather(proj, "x", axis=0)

    other = other.reshape(blocks, -1, width)
    own = swap(other, "x")
    chosen = join_rows(jnp.where(before, other, own), "zl")
    chosen = spread(chosen, "y")
    chosen, proj_blocks = lax.optimization_barrier((chosen, proj_blocks))
    chosen = spread(chosen, "core")

    shares = pl.pallas_call(
        partial_kernel,
        out_shape=jax.ShapeDtypeStruct((blocks, rows, width), BF16),
        in_specs=[SMEM] + [VMEM] * 4,
        out_specs=VMEM,
        compiler_params=PARAMS,
    )(here, vector, chosen, proj_blocks, own_map)
    shares = swap(shares, "x")
    dedge, sums = pl.pallas_call(
        edge_kernel,
        out_shape=(
            jax.ShapeDtypeStruct((rows, width), F32),
            jax.ShapeDtypeStruct((8, 128), F32),
        ),
        in_specs=[VMEM, VMEM],
        out_specs=(VMEM, VMEM),
        compiler_params=PARAMS,
    )(vector, shares)
    for axis in ("core", "x", "y", "zl"):
        sums = lax.psum(sums, axis)
    sums = spread(sums, "zh")
    return pl.pallas_call(
        functools.partial(finish_kernel, float(rows_total * bond)),
        out_shape=(
            jax.ShapeDtypeStruct((rows, width), F32),
            jax.ShapeDtypeStruct((2,), F32),
        ),
        in_specs=[VMEM] * 3,
        out_specs=(VMEM, SMEM),
        compiler_params=PARAMS,
    )(sums, vector, dedge)


def solution(mesh):
    fine = Mesh(mesh.devices.reshape(4, 4, -1, 2, mesh.shape["col"]), ROW + ("x",))
    in_specs = (P(ROW, "x"), P(None, "x"), P(None, "x"), P(ROW, "x"))
    out_specs = (P(ROW, "x"), P())
    return jax.shard_map(
        on_device, mesh=fine, in_specs=in_specs, out_specs=out_specs, check_vma=False
    )
```

```python
import functools

import jax
import jax.numpy as jnp
from jax import lax
from jax.experimental import pallas as pl
from jax.experimental.pallas import tpu as pltpu
from jax.sharding import Mesh, PartitionSpec as P

BF16 = jnp.bfloat16
F32 = jnp.float32
ROW = ("y", "zh", "zl", "core")
VMEM = pl.BlockSpec(memory_space=pltpu.VMEM)
SMEM = pl.BlockSpec(memory_space=pltpu.SMEM)
PARAMS = pltpu.CompilerParams(vmem_limit_bytes=10 * 1024 * 1024)


def swap(pieces, axis):
    return lax.all_to_all(pieces, axis, split_axis=0, concat_axis=0, tiled=True)


def spread(block, axis):
    members = lax.axis_size(axis)
    return swap(jnp.broadcast_to(block[None], (members, *block.shape)), axis)


def total(pieces):
    return jnp.sum(pieces.astype(F32), axis=0)


def scatter_sum(block, axis):
    members = lax.axis_size(axis)
    pieces = block.reshape(members, block.shape[0] // members, block.shape[1])
    return total(swap(pieces, axis))


def join_rows(blocks, axis):
    stacked = spread(blocks, axis)
    members, count, rows, width = stacked.shape
    return stacked.transpose(1, 0, 2, 3).reshape(count, members * rows, width)


def dot(a, b):
    return jnp.dot(a, b, preferred_element_type=F32)


def dot_turned(a, b):
    return lax.dot_general(a, b, (((1,), (1,)), ((), ())), preferred_element_type=F32)


def partial_kernel(place, vec, sym, proj, own_map, out):
    rows, width = vec.shape
    blocks = proj.shape[0]
    first = lax.broadcasted_iota(jnp.int32, (width, width), 0)
    second = lax.broadcasted_iota(jnp.int32, (width, width), 1)
    zero = jnp.zeros((width, width), BF16)
    acc = jnp.zeros((rows, width), F32)
    for k in range(blocks):
        shift = (place[0] - k) * width
        block = jnp.concatenate(
            [sym[c, y, k] for c in range(sym.shape[0]) for y in range(sym.shape[1])]
        )
        part = proj[k, :rows]
        acc += dot(part, jnp.where(first <= second + shift, block, zero))
        acc += dot_turned(part, jnp.where(first < second - shift, block, zero))
    corrected = (vec[...] - acc).astype(BF16)
    for k in range(blocks):
        share = dot_turned(corrected, own_map[k * width : (k + 1) * width])
        out[k] = share.astype(BF16)


def fold(values):
    line = jnp.sum(values, axis=0, keepdims=True)
    return sum(line[:, i : i + 128] for i in range(0, values.shape[1], 128))


def edge_kernel(vec, shares, dedge, sums):
    acc = sum(shares[k].astype(F32) for k in range(shares.shape[0]))
    v = vec[...]
    dedge[...] = acc
    sums[...] = jnp.concatenate(
        [fold(v * v), fold(v * acc), fold(acc * acc), jnp.zeros((5, 128), F32)], axis=0
    )


def finish_kernel(count, sums, vec, dedge, out, coeffs):
    vv, vd, dd = (jnp.sum(sums[i : i + 1], axis=1, keepdims=True) for i in range(3))
    along = (vv - vd) / count
    keep = 1.0 - along
    square = (keep * keep * vv - 2.0 * keep * vd + dd) / count
    scale = jnp.sqrt(jnp.maximum(square, 0.0) + 1e-06)
    inverse = 1.0 / scale
    out[...] = (keep * vec[...] - dedge[...]) * inverse
    coeffs[0] = along[0, 0]
    coeffs[1] = scale[0, 0]


def on_device(edge, corner, tri_inv, vector):
    bond, width = corner.shape
    rows = vector.shape[0]
    blocks = bond // width
    place = lax.axis_index("x")
    here = place[None]
    rows_total = rows * lax.axis_size(ROW)

    before = lax.broadcasted_iota(jnp.int32, (blocks, 1, 1), 0) < place
    edge, here, before = lax.optimization_barrier((edge, here, before))
    corner_wide = lax.all_gather(corner, "x", axis=1, tiled=True)
    edge_wide = lax.all_gather(edge, "x", axis=1, tiled=True)
    vec_low = vector.astype(BF16)
    cross = lax.dot_general(
        vec_low, edge_wide, (((0,), (0,)), ((), ())), preferred_element_type=F32
    )
    cross = cross * (1.0 / rows_total)
    for axis in ("core", "y", "zl"):
        cross = scatter_sum(cross.astype(BF16), axis)
    cross = total(spread(cross.astype(BF16), "zh")).astype(BF16)
    cross_all = spread(cross, "x").reshape(-1, bond)

    own_map = dot(corner_wide, tri_inv).astype(BF16)
    proj = dot(edge_wide, own_map).astype(BF16)
    proj = jnp.concatenate([proj, own_map[: width - rows]])
    proj_blocks = lax.all_gather(proj, "x", axis=0)

    other = dot(cross_all, own_map).astype(BF16).reshape(blocks, -1, width)
    own = swap(other, "x")
    chosen = join_rows(jnp.where(before, other, own), "zl")
    chosen = spread(chosen, "y")
    chosen, proj_blocks = lax.optimization_barrier((chosen, proj_blocks))
    chosen = spread(chosen, "core")

    shares = pl.pallas_call(
        partial_kernel,
        out_shape=jax.ShapeDtypeStruct((blocks, rows, width), BF16),
        in_specs=[SMEM] + [VMEM] * 4,
        out_specs=VMEM,
        compiler_params=PARAMS,
    )(here, vector, chosen, proj_blocks, own_map)
    shares = swap(shares, "x")
    dedge, sums = pl.pallas_call(
        edge_kernel,
        out_shape=(
            jax.ShapeDtypeStruct((rows, width), F32),
            jax.ShapeDtypeStruct((8, 128), F32),
        ),
        in_specs=[VMEM, VMEM],
        out_specs=(VMEM, VMEM),
        compiler_params=PARAMS,
    )(vector, shares)
    sums = lax.psum(sums, "core")
    for axis in ("x", "y", "zl"):
        sums = total(spread(sums, axis))
    sums = lax.psum(sums, "zh")
    return pl.pallas_call(
        functools.partial(finish_kernel, float(rows_total * bond)),
        out_shape=(
            jax.ShapeDtypeStruct((rows, width), F32),
            jax.ShapeDtypeStruct((2,), F32),
        ),
        in_specs=[VMEM] * 3,
        out_specs=(VMEM, SMEM),
        compiler_params=PARAMS,
    )(sums, vector, dedge)


def solution(mesh):
    fine = Mesh(mesh.devices.reshape(4, 4, -1, 2, mesh.shape["col"]), ROW + ("x",))
    in_specs = (P(ROW, "x"), P(None, "x"), P(None, "x"), P(ROW, "x"))
    out_specs = (P(ROW, "x"), P())
    return jax.shard_map(
        on_device, mesh=fine, in_specs=in_specs, out_specs=out_specs, check_vma=False
    )
```

```python
import functools

import jax
import jax.numpy as jnp
from jax import lax
from jax.experimental import pallas as pl
from jax.experimental.pallas import tpu as pltpu
from jax.sharding import Mesh, PartitionSpec as P

BF16 = jnp.bfloat16
F32 = jnp.float32
ROW = ("y", "zh", "zl", "core")
VMEM = pl.BlockSpec(memory_space=pltpu.VMEM)
SMEM = pl.BlockSpec(memory_space=pltpu.SMEM)
PARAMS = pltpu.CompilerParams(vmem_limit_bytes=10 * 1024 * 1024)


def swap(pieces, axis):
    return lax.all_to_all(pieces, axis, split_axis=0, concat_axis=0, tiled=True)


def spread(block, axis):
    members = lax.axis_size(axis)
    return swap(jnp.broadcast_to(block[None], (members, *block.shape)), axis)


def total(pieces):
    return jnp.sum(pieces.astype(F32), axis=0)


def scatter_sum(block, axis):
    members = lax.axis_size(axis)
    pieces = block.reshape(members, block.shape[0] // members, block.shape[1])
    return total(swap(pieces, axis))


def join_rows(blocks, axis):
    stacked = spread(blocks, axis)
    members, count, rows, width = stacked.shape
    return stacked.transpose(1, 0, 2, 3).reshape(count, members * rows, width)


def dot(a, b):
    return jnp.dot(a, b, preferred_element_type=F32)


def dot_turned(a, b):
    return lax.dot_general(a, b, (((1,), (1,)), ((), ())), preferred_element_type=F32)


def add_kernel(pieces, out):
    out[...] = sum(pieces[i].astype(F32) for i in range(pieces.shape[0])).astype(BF16)


def proj_kernel(edge, own_map, out):
    rows = edge.shape[0]
    out[:rows] = dot(edge[...], own_map[...]).astype(BF16)
    out[rows:] = jnp.zeros((out.shape[0] - rows, out.shape[1]), BF16)


def partial_kernel(place, vec, sym, proj, own_map, out):
    rows, width = vec.shape
    blocks = proj.shape[0]
    first = lax.broadcasted_iota(jnp.int32, (width, width), 0)
    second = lax.broadcasted_iota(jnp.int32, (width, width), 1)
    zero = jnp.zeros((width, width), BF16)
    acc = jnp.zeros((rows, width), F32)
    for k in range(blocks):
        shift = (place[0] - k) * width
        block = jnp.concatenate(
            [sym[c, y, k] for c in range(sym.shape[0]) for y in range(sym.shape[1])]
        )
        part = proj[k, :rows]
        acc += dot(part, jnp.where(first <= second + shift, block, zero))
        acc += dot_turned(part, jnp.where(first < second - shift, block, zero))
    corrected = (vec[...] - acc).astype(BF16)
    for k in range(blocks):
        share = dot_turned(corrected, own_map[k * width : (k + 1) * width])
        out[k] = share.astype(BF16)


def fold(values):
    line = jnp.sum(values, axis=0, keepdims=True)
    return sum(line[:, i : i + 128] for i in range(0, values.shape[1], 128))


def edge_kernel(vec, shares, dedge, sums):
    acc = sum(shares[k].astype(F32) for k in range(shares.shape[0]))
    v = vec[...]
    dedge[...] = acc
    sums[...] = jnp.concatenate(
        [fold(v * v), fold(v * acc), fold(acc * acc), jnp.zeros((5, 128), F32)], axis=0
    )


def finish_kernel(count, sums, vec, dedge, out, coeffs):
    vv, vd, dd = (jnp.sum(sums[i : i + 1], axis=1, keepdims=True) for i in range(3))
    along = (vv - vd) / count
    keep = 1.0 - along
    square = (keep * keep * vv - 2.0 * keep * vd + dd) / count
    scale = jnp.sqrt(jnp.maximum(square, 0.0) + 1e-06)
    inverse = 1.0 / scale
    out[...] = (keep * vec[...] - dedge[...]) * inverse
    coeffs[0] = along[0, 0]
    coeffs[1] = scale[0, 0]


def on_device(edge, corner, tri_inv, vector):
    bond, width = corner.shape
    rows = vector.shape[0]
    blocks = bond // width
    place = lax.axis_index("x")
    here = place[None]
    rows_total = rows * lax.axis_size(ROW)

    before = lax.broadcasted_iota(jnp.int32, (blocks, 1, 1), 0) < place
    edge, here, before = lax.optimization_barrier((edge, here, before))
    corner_wide = lax.all_gather(corner, "x", axis=1, tiled=True)
    edge_wide = lax.all_gather(edge, "x", axis=1, tiled=True)
    vec_low = vector.astype(BF16)
    cross = lax.dot_general(
        vec_low, edge_wide, (((0,), (0,)), ((), ())), preferred_element_type=F32
    )
    cross = cross * (1.0 / rows_total)
    pair = swap(cross.astype(BF16).reshape(2, -1, bond), "core")
    cross = pl.pallas_call(
        add_kernel,
        out_shape=jax.ShapeDtypeStruct(pair.shape[1:], BF16),
        in_specs=[VMEM],
        out_specs=VMEM,
        compiler_params=PARAMS,
    )(pair)
    for axis in ("y", "zl"):
        cross = scatter_sum(cross.astype(BF16), axis)
    cross = total(spread(cross.astype(BF16), "zh")).astype(BF16)
    cross_all = spread(cross, "x").reshape(-1, bond)

    own_map = dot(corner_wide, tri_inv).astype(BF16)
    proj = pl.pallas_call(
        proj_kernel,
        out_shape=jax.ShapeDtypeStruct((width, width), BF16),
        in_specs=[VMEM, VMEM],
        out_specs=VMEM,
        compiler_params=PARAMS,
        cost_estimate=pl.CostEstimate(
            flops=2 * rows * bond * width,
            bytes_accessed=2 * bond * (rows + width),
            transcendentals=0,
        ),
    )(edge_wide, own_map)
    proj_blocks = lax.all_gather(proj, "x", axis=0)

    other = dot(cross_all, own_map).astype(BF16).reshape(blocks, -1, width)
    own = swap(other, "x")
    chosen = join_rows(jnp.where(before, other, own), "zl")
    chosen = spread(chosen, "y")
    chosen, proj_blocks = lax.optimization_barrier((chosen, proj_blocks))
    chosen = spread(chosen, "core")

    shares = pl.pallas_call(
        partial_kernel,
        out_shape=jax.ShapeDtypeStruct((blocks, rows, width), BF16),
        in_specs=[SMEM] + [VMEM] * 4,
        out_specs=VMEM,
        compiler_params=PARAMS,
    )(here, vector, chosen, proj_blocks, own_map)
    shares = swap(shares, "x")
    dedge, sums = pl.pallas_call(
        edge_kernel,
        out_shape=(
            jax.ShapeDtypeStruct((rows, width), F32),
            jax.ShapeDtypeStruct((8, 128), F32),
        ),
        in_specs=[VMEM, VMEM],
        out_specs=(VMEM, VMEM),
        compiler_params=PARAMS,
    )(vector, shares)
    sums = lax.psum(sums, "core")
    for axis in ("x", "y", "zl"):
        sums = total(spread(sums, axis))
    sums = lax.psum(sums, "zh")
    return pl.pallas_call(
        functools.partial(finish_kernel, float(rows_total * bond)),
        out_shape=(
            jax.ShapeDtypeStruct((rows, width), F32),
            jax.ShapeDtypeStruct((2,), F32),
        ),
        in_specs=[VMEM] * 3,
        out_specs=(VMEM, SMEM),
        compiler_params=PARAMS,
    )(sums, vector, dedge)


def solution(mesh):
    fine = Mesh(mesh.devices.reshape(4, 4, -1, 2, mesh.shape["col"]), ROW + ("x",))
    in_specs = (P(ROW, "x"), P(None, "x"), P(None, "x"), P(ROW, "x"))
    out_specs = (P(ROW, "x"), P())
    return jax.shard_map(
        on_device, mesh=fine, in_specs=in_specs, out_specs=out_specs, check_vma=False
    )
```

```python
import functools

import jax
import jax.numpy as jnp
from jax import lax
from jax.experimental import pallas as pl
from jax.experimental.pallas import tpu as pltpu
from jax.sharding import Mesh, PartitionSpec as P

BF16 = jnp.bfloat16
F32 = jnp.float32
ROW = ("y", "zh", "zl", "core")
VMEM = pl.BlockSpec(memory_space=pltpu.VMEM)
SMEM = pl.BlockSpec(memory_space=pltpu.SMEM)
PARAMS = pltpu.CompilerParams(vmem_limit_bytes=10 * 1024 * 1024)


def swap(pieces, axis):
    return lax.all_to_all(pieces, axis, split_axis=0, concat_axis=0, tiled=True)


def spread(block, axis):
    members = lax.axis_size(axis)
    return swap(jnp.broadcast_to(block[None], (members, *block.shape)), axis)


def total(pieces):
    return jnp.sum(pieces.astype(F32), axis=0)


def scatter_sum(block, axis):
    members = lax.axis_size(axis)
    pieces = block.reshape(members, block.shape[0] // members, block.shape[1])
    return total(swap(pieces, axis))


def join_rows(blocks, axis):
    stacked = spread(blocks, axis)
    members, count, rows, width = stacked.shape
    return stacked.transpose(1, 0, 2, 3).reshape(count, members * rows, width)


def dot(a, b):
    return jnp.dot(a, b, preferred_element_type=F32)


def dot_turned(a, b):
    return lax.dot_general(a, b, (((1,), (1,)), ((), ())), preferred_element_type=F32)


def add_kernel(pieces, out):
    out[...] = sum(pieces[i].astype(F32) for i in range(pieces.shape[0])).astype(BF16)


def proj_kernel(edge, own_map, out):
    rows = edge.shape[0]
    out[:rows] = dot(edge[...], own_map[...]).astype(BF16)
    out[rows:] = jnp.zeros((out.shape[0] - rows, out.shape[1]), BF16)


def partial_kernel(place, vec, sym, proj, own_map, out):
    rows, width = vec.shape
    blocks = proj.shape[0]
    first = lax.broadcasted_iota(jnp.int32, (width, width), 0)
    second = lax.broadcasted_iota(jnp.int32, (width, width), 1)
    zero = jnp.zeros((width, width), BF16)
    acc = jnp.zeros((rows, width), F32)
    for k in range(blocks):
        shift = (place[0] - k) * width
        block = jnp.concatenate(
            [sym[c, y, k] for c in range(sym.shape[0]) for y in range(sym.shape[1])]
        )
        part = proj[k, :rows]
        acc += dot(part, jnp.where(first <= second + shift, block, zero))
        acc += dot_turned(part, jnp.where(first < second - shift, block, zero))
    corrected = (vec[...] - acc).astype(BF16)
    for k in range(blocks):
        share = dot_turned(corrected, own_map[k * width : (k + 1) * width])
        out[k] = share.astype(BF16)


def fold(values):
    line = jnp.sum(values, axis=0, keepdims=True)
    return sum(line[:, i : i + 128] for i in range(0, values.shape[1], 128))


def edge_kernel(vec, shares, dedge, sums):
    acc = sum(shares[k].astype(F32) for k in range(shares.shape[0]))
    v = vec[...]
    dedge[...] = acc
    sums[...] = jnp.concatenate(
        [fold(v * v), fold(v * acc), fold(acc * acc), jnp.zeros((5, 128), F32)], axis=0
    )


def finish_kernel(count, sums, vec, dedge, out, coeffs):
    lines = sum(sums[i] for i in range(sums.shape[0]))
    vv, vd, dd = (jnp.sum(lines[i : i + 1], axis=1, keepdims=True) for i in range(3))
    along = (vv - vd) / count
    keep = 1.0 - along
    square = (keep * keep * vv - 2.0 * keep * vd + dd) / count
    scale = jnp.sqrt(jnp.maximum(square, 0.0) + 1e-06)
    inverse = 1.0 / scale
    out[...] = (keep * vec[...] - dedge[...]) * inverse
    coeffs[0] = along[0, 0]
    coeffs[1] = scale[0, 0]


def on_device(edge, corner, tri_inv, vector):
    bond, width = corner.shape
    rows = vector.shape[0]
    blocks = bond // width
    place = lax.axis_index("x")
    here = place[None]
    rows_total = rows * lax.axis_size(ROW)

    before = lax.broadcasted_iota(jnp.int32, (blocks, 1, 1), 0) < place
    edge, here, before = lax.optimization_barrier((edge, here, before))
    corner_wide = lax.all_gather(corner, "x", axis=1, tiled=True)
    edge_wide = lax.all_gather(edge, "x", axis=1, tiled=True)
    vec_low = vector.astype(BF16)
    cross = lax.dot_general(
        vec_low, edge_wide, (((0,), (0,)), ((), ())), preferred_element_type=F32
    )
    cross = cross * (1.0 / rows_total)
    pair = swap(cross.astype(BF16).reshape(2, -1, bond), "core")
    cross = pl.pallas_call(
        add_kernel,
        out_shape=jax.ShapeDtypeStruct(pair.shape[1:], BF16),
        in_specs=[VMEM],
        out_specs=VMEM,
        compiler_params=PARAMS,
    )(pair)
    for axis in ("y", "zl"):
        cross = scatter_sum(cross.astype(BF16), axis)
    cross = total(spread(cross.astype(BF16), "zh")).astype(BF16)
    cross_all = spread(cross, "x").reshape(-1, bond)

    own_map = dot(corner_wide, tri_inv).astype(BF16)
    proj = pl.pallas_call(
        proj_kernel,
        out_shape=jax.ShapeDtypeStruct((width, width), BF16),
        in_specs=[VMEM, VMEM],
        out_specs=VMEM,
        compiler_params=PARAMS,
        cost_estimate=pl.CostEstimate(
            flops=2 * rows * bond * width,
            bytes_accessed=2 * bond * (rows + width),
            transcendentals=0,
        ),
    )(edge_wide, own_map)
    proj_blocks = lax.all_gather(proj, "x", axis=0)

    other = dot(cross_all, own_map).astype(BF16).reshape(blocks, -1, width)
    own = swap(other, "x")
    chosen = join_rows(jnp.where(before, other, own), "zl")
    chosen = spread(chosen, "y")
    chosen, proj_blocks = lax.optimization_barrier((chosen, proj_blocks))
    chosen = spread(chosen, "core")

    shares = pl.pallas_call(
        partial_kernel,
        out_shape=jax.ShapeDtypeStruct((blocks, rows, width), BF16),
        in_specs=[SMEM] + [VMEM] * 4,
        out_specs=VMEM,
        compiler_params=PARAMS,
    )(here, vector, chosen, proj_blocks, own_map)
    shares = swap(shares, "x")
    dedge, sums = pl.pallas_call(
        edge_kernel,
        out_shape=(
            jax.ShapeDtypeStruct((rows, width), F32),
            jax.ShapeDtypeStruct((8, 128), F32),
        ),
        in_specs=[VMEM, VMEM],
        out_specs=(VMEM, VMEM),
        compiler_params=PARAMS,
    )(vector, shares)
    sums = total(spread(sums, ("y", "core", "x")))
    sums = spread(sums, ("zh", "zl"))
    return pl.pallas_call(
        functools.partial(finish_kernel, float(rows_total * bond)),
        out_shape=(
            jax.ShapeDtypeStruct((rows, width), F32),
            jax.ShapeDtypeStruct((2,), F32),
        ),
        in_specs=[VMEM] * 3,
        out_specs=(VMEM, SMEM),
        compiler_params=PARAMS,
    )(sums, vector, dedge)


def solution(mesh):
    fine = Mesh(mesh.devices.reshape(4, 4, -1, 2, mesh.shape["col"]), ROW + ("x",))
    in_specs = (P(ROW, "x"), P(None, "x"), P(None, "x"), P(ROW, "x"))
    out_specs = (P(ROW, "x"), P())
    return jax.shard_map(
        on_device, mesh=fine, in_specs=in_specs, out_specs=out_specs, check_vma=False
    )
```

```python
import functools

import jax
import jax.numpy as jnp
from jax import lax
from jax.experimental import pallas as pl
from jax.experimental.pallas import tpu as pltpu
from jax.sharding import Mesh, PartitionSpec as P

BF16 = jnp.bfloat16
F32 = jnp.float32
ROW = ("y", "zh", "zl", "core")
VMEM = pl.BlockSpec(memory_space=pltpu.VMEM)
SMEM = pl.BlockSpec(memory_space=pltpu.SMEM)
PARAMS = pltpu.CompilerParams(vmem_limit_bytes=10 * 1024 * 1024)
LARGE = pltpu.CompilerParams(vmem_limit_bytes=56 * 1024 * 1024)


def swap(pieces, axis):
    return lax.all_to_all(pieces, axis, split_axis=0, concat_axis=0, tiled=True)


def spread(block, axis):
    members = lax.axis_size(axis)
    return swap(jnp.broadcast_to(block[None], (members, *block.shape)), axis)


def total(pieces):
    return jnp.sum(pieces.astype(F32), axis=0)


def scatter_sum(block, axis):
    members = lax.axis_size(axis)
    pieces = block.reshape(members, block.shape[0] // members, block.shape[1])
    return total(swap(pieces, axis))


def join_rows(blocks, axis):
    stacked = spread(blocks, axis)
    members, count, rows, width = stacked.shape
    return stacked.transpose(1, 0, 2, 3).reshape(count, members * rows, width)


def dot(a, b):
    return jnp.dot(a, b, preferred_element_type=F32)


def dot_turned(a, b):
    return lax.dot_general(a, b, (((1,), (1,)), ((), ())), preferred_element_type=F32)


def cross_kernel(scale, vec, edge, out):
    width = vec.shape[1]
    turned = vec[...].T.astype(BF16)
    for k in range(edge.shape[0]):
        out[:, k * width : (k + 1) * width] = (dot(turned, edge[k]) * scale).astype(BF16)


def add_kernel(pieces, out):
    out[...] = sum(pieces[i].astype(F32) for i in range(pieces.shape[0])).astype(BF16)


def map_kernel(corner, tri_inv, edge, own_map, proj, acc):
    step = pl.program_id(0)
    blocks, _, width = corner.shape
    rows = edge.shape[1]

    @pl.when(step == 0)
    def _():
        acc[...] = jnp.zeros_like(acc)
        proj[rows:] = jnp.zeros((proj.shape[0] - rows, proj.shape[1]), BF16)

    own_map[...] = sum(
        dot(corner[k], tri_inv[k * width : (k + 1) * width]) for k in range(blocks)
    ).astype(BF16)
    acc[...] += dot(edge[0], own_map[...])

    @pl.when(step == pl.num_programs(0) - 1)
    def _():
        proj[:rows] = acc[...].astype(BF16)


def partial_kernel(place, vec, sym, proj, own_map, out):
    rows, width = vec.shape
    blocks = proj.shape[0]
    first = lax.broadcasted_iota(jnp.int32, (width, width), 0)
    second = lax.broadcasted_iota(jnp.int32, (width, width), 1)
    zero = jnp.zeros((width, width), BF16)
    acc = jnp.zeros((rows, width), F32)
    for k in range(blocks):
        shift = (place[0] - k) * width
        block = jnp.concatenate(
            [sym[c, y, k] for c in range(sym.shape[0]) for y in range(sym.shape[1])]
        )
        part = proj[k, :rows]
        acc += dot(part, jnp.where(first <= second + shift, block, zero))
        acc += dot_turned(part, jnp.where(first < second - shift, block, zero))
    corrected = (vec[...] - acc).astype(BF16)
    for k in range(blocks):
        share = dot_turned(corrected, own_map[k * width : (k + 1) * width])
        out[k] = share.astype(BF16)


def fold(values):
    line = jnp.sum(values, axis=0, keepdims=True)
    return sum(line[:, i : i + 128] for i in range(0, values.shape[1], 128))


def edge_kernel(vec, shares, dedge, sums):
    acc = sum(shares[k].astype(F32) for k in range(shares.shape[0]))
    v = vec[...]
    dedge[...] = acc
    sums[...] = jnp.concatenate(
        [fold(v * v), fold(v * acc), fold(acc * acc), jnp.zeros((5, 128), F32)], axis=0
    )


def finish_kernel(count, sums, vec, dedge, out, coeffs):
    lines = sum(sums[i] for i in range(sums.shape[0]))
    vv, vd, dd = (jnp.sum(lines[i : i + 1], axis=1, keepdims=True) for i in range(3))
    along = (vv - vd) / count
    keep = 1.0 - along
    square = (keep * keep * vv - 2.0 * keep * vd + dd) / count
    scale = jnp.sqrt(jnp.maximum(square, 0.0) + 1e-06)
    inverse = 1.0 / scale
    out[...] = (keep * vec[...] - dedge[...]) * inverse
    coeffs[0] = along[0, 0]
    coeffs[1] = scale[0, 0]


def on_device(edge, corner, tri_inv, vector):
    bond, width = corner.shape
    rows = vector.shape[0]
    blocks = bond // width
    place = lax.axis_index("x")
    here = place[None]
    rows_total = rows * lax.axis_size(ROW)

    before = lax.broadcasted_iota(jnp.int32, (blocks, 1, 1), 0) < place
    edge, here, before = lax.optimization_barrier((edge, here, before))
    corner_blocks = lax.all_gather(corner, "x", axis=0)
    edge_blocks = spread(edge, "x")
    cross = pl.pallas_call(
        functools.partial(cross_kernel, 1.0 / rows_total),
        out_shape=jax.ShapeDtypeStruct((width, bond), BF16),
        in_specs=[VMEM, VMEM],
        out_specs=VMEM,
        compiler_params=PARAMS,
    )(vector, edge_blocks)
    pair = swap(cross.reshape(2, -1, bond), "core")
    cross = pl.pallas_call(
        add_kernel,
        out_shape=jax.ShapeDtypeStruct(pair.shape[1:], BF16),
        in_specs=[VMEM],
        out_specs=VMEM,
        compiler_params=PARAMS,
    )(pair)
    for axis in ("y", "zl"):
        cross = scatter_sum(cross.astype(BF16), axis)
    cross = total(spread(cross.astype(BF16), "zh")).astype(BF16)
    cross_all = spread(cross, "x").reshape(-1, bond)

    own_map, proj = pl.pallas_call(
        map_kernel,
        grid=(blocks,),
        out_shape=(
            jax.ShapeDtypeStruct((bond, width), BF16),
            jax.ShapeDtypeStruct((width, width), BF16),
        ),
        in_specs=[
            pl.BlockSpec((blocks, width, width), lambda i: (0, i, 0)),
            pl.BlockSpec((bond, width), lambda i: (0, 0)),
            pl.BlockSpec((1, rows, width), lambda i: (i, 0, 0)),
        ],
        out_specs=(
            pl.BlockSpec((width, width), lambda i: (i, 0)),
            pl.BlockSpec((width, width), lambda i: (0, 0)),
        ),
        scratch_shapes=[pltpu.VMEM((rows, width), F32)],
        compiler_params=LARGE,
        cost_estimate=pl.CostEstimate(
            flops=2 * (bond + rows) * bond * width,
            bytes_accessed=2 * bond * (bond + 2 * width),
            transcendentals=0,
        ),
    )(corner_blocks, tri_inv, edge_blocks)
    proj_blocks = lax.all_gather(proj, "x", axis=0)

    other = dot(cross_all, own_map).astype(BF16).reshape(blocks, -1, width)
    own = swap(other, "x")
    chosen = join_rows(jnp.where(before, other, own), "zl")
    chosen = spread(chosen, "y")
    chosen, proj_blocks = lax.optimization_barrier((chosen, proj_blocks))
    chosen = spread(chosen, "core")

    shares = pl.pallas_call(
        partial_kernel,
        out_shape=jax.ShapeDtypeStruct((blocks, rows, width), BF16),
        in_specs=[SMEM] + [VMEM] * 4,
        out_specs=VMEM,
        compiler_params=PARAMS,
    )(here, vector, chosen, proj_blocks, own_map)
    shares = swap(shares, "x")
    dedge, sums = pl.pallas_call(
        edge_kernel,
        out_shape=(
            jax.ShapeDtypeStruct((rows, width), F32),
            jax.ShapeDtypeStruct((8, 128), F32),
        ),
        in_specs=[VMEM, VMEM],
        out_specs=(VMEM, VMEM),
        compiler_params=PARAMS,
    )(vector, shares)
    sums = total(spread(sums, ("y", "core", "x")))
    sums = spread(sums, ("zh", "zl"))
    return pl.pallas_call(
        functools.partial(finish_kernel, float(rows_total * bond)),
        out_shape=(
            jax.ShapeDtypeStruct((rows, width), F32),
            jax.ShapeDtypeStruct((2,), F32),
        ),
        in_specs=[VMEM] * 3,
        out_specs=(VMEM, SMEM),
        compiler_params=PARAMS,
    )(sums, vector, dedge)


def solution(mesh):
    fine = Mesh(mesh.devices.reshape(4, 4, -1, 2, mesh.shape["col"]), ROW + ("x",))
    in_specs = (P(ROW, "x"), P(None, "x"), P(None, "x"), P(ROW, "x"))
    out_specs = (P(ROW, "x"), P())
    return jax.shard_map(
        on_device, mesh=fine, in_specs=in_specs, out_specs=out_specs, check_vma=False
    )
```

```python
import functools

import jax
import jax.numpy as jnp
from jax import lax
from jax.experimental import pallas as pl
from jax.experimental.pallas import tpu as pltpu
from jax.sharding import Mesh, PartitionSpec as P

BF16 = jnp.bfloat16
F32 = jnp.float32
ROW = ("y", "zh", "zl", "core")
VMEM = pl.BlockSpec(memory_space=pltpu.VMEM)
SMEM = pl.BlockSpec(memory_space=pltpu.SMEM)
PARAMS = pltpu.CompilerParams(vmem_limit_bytes=10 * 1024 * 1024)
LARGE = pltpu.CompilerParams(vmem_limit_bytes=56 * 1024 * 1024)


def swap(pieces, axis):
    return lax.all_to_all(pieces, axis, split_axis=0, concat_axis=0, tiled=True)


def spread(block, axis):
    members = lax.axis_size(axis)
    return swap(jnp.broadcast_to(block[None], (members, *block.shape)), axis)


def total(pieces):
    return jnp.sum(pieces.astype(F32), axis=0)


def scatter_sum(block, axis):
    members = lax.axis_size(axis)
    pieces = block.reshape(members, block.shape[0] // members, block.shape[1])
    return total(swap(pieces, axis))


def join_rows(blocks, axis):
    stacked = spread(blocks, axis)
    members, count, rows, width = stacked.shape
    return stacked.transpose(1, 0, 2, 3).reshape(count, members * rows, width)


def dot(a, b):
    return jnp.dot(a, b, preferred_element_type=F32)


def dot_turned(a, b):
    return lax.dot_general(a, b, (((1,), (1,)), ((), ())), preferred_element_type=F32)


def add_kernel(pieces, out):
    out[...] = sum(pieces[i].astype(F32) for i in range(pieces.shape[0])).astype(BF16)


def proj_kernel(edge, own_map, out):
    rows = edge.shape[0]
    out[:rows] = dot(edge[...], own_map[...]).astype(BF16)
    out[rows:] = jnp.zeros((out.shape[0] - rows, out.shape[1]), BF16)


def partial_kernel(place, vec, sym, proj, own_map, out):
    rows, width = vec.shape
    blocks = proj.shape[0]
    first = lax.broadcasted_iota(jnp.int32, (width, width), 0)
    second = lax.broadcasted_iota(jnp.int32, (width, width), 1)
    zero = jnp.zeros((width, width), BF16)
    acc = jnp.zeros((rows, width), F32)
    for k in range(blocks):
        shift = (place[0] - k) * width
        block = jnp.concatenate(
            [sym[c, y, k] for c in range(sym.shape[0]) for y in range(sym.shape[1])]
        )
        part = proj[k, :rows]
        acc += dot(part, jnp.where(first <= second + shift, block, zero))
        acc += dot_turned(part, jnp.where(first < second - shift, block, zero))
    corrected = (vec[...] - acc).astype(BF16)
    for k in range(blocks):
        share = dot_turned(corrected, own_map[k * width : (k + 1) * width])
        out[k] = share.astype(BF16)


def fold(values):
    line = jnp.sum(values, axis=0, keepdims=True)
    return sum(line[:, i : i + 128] for i in range(0, values.shape[1], 128))


def edge_kernel(vec, shares, dedge, sums):
    acc = sum(shares[k].astype(F32) for k in range(shares.shape[0]))
    v = vec[...]
    dedge[...] = acc
    sums[...] = jnp.concatenate(
        [fold(v * v), fold(v * acc), fold(acc * acc), jnp.zeros((5, 128), F32)], axis=0
    )


def finish_kernel(count, sums, vec, dedge, out, coeffs):
    lines = sum(sums[i] for i in range(sums.shape[0]))
    vv, vd, dd = (jnp.sum(lines[i : i + 1], axis=1, keepdims=True) for i in range(3))
    along = (vv - vd) / count
    keep = 1.0 - along
    square = (keep * keep * vv - 2.0 * keep * vd + dd) / count
    scale = jnp.sqrt(jnp.maximum(square, 0.0) + 1e-06)
    inverse = 1.0 / scale
    out[...] = (keep * vec[...] - dedge[...]) * inverse
    coeffs[0] = along[0, 0]
    coeffs[1] = scale[0, 0]


def on_device(edge, corner, tri_inv, vector):
    bond, width = corner.shape
    rows = vector.shape[0]
    blocks = bond // width
    place = lax.axis_index("x")
    here = place[None]
    rows_total = rows * lax.axis_size(ROW)

    before = lax.broadcasted_iota(jnp.int32, (blocks, 1, 1), 0) < place
    edge, here, before = lax.optimization_barrier((edge, here, before))
    corner_wide = lax.all_gather(corner, "x", axis=1, tiled=True)
    edge_wide = lax.all_gather(edge, "x", axis=1, tiled=True)
    vec_low = vector.astype(BF16)
    cross = lax.dot_general(
        vec_low, edge_wide, (((0,), (0,)), ((), ())), preferred_element_type=F32
    )
    cross = cross * (1.0 / rows_total)
    pair = swap(cross.astype(BF16).reshape(2, -1, bond), "core")
    cross = pl.pallas_call(
        add_kernel,
        out_shape=jax.ShapeDtypeStruct(pair.shape[1:], BF16),
        in_specs=[VMEM],
        out_specs=VMEM,
        compiler_params=PARAMS,
    )(pair)
    for axis in ("y", "zl"):
        cross = scatter_sum(cross.astype(BF16), axis)
    cross = total(spread(cross.astype(BF16), "zh")).astype(BF16)
    cross_all = spread(cross, "x").reshape(-1, bond)

    own_map = dot(corner_wide, tri_inv).astype(BF16)
    proj = pl.pallas_call(
        proj_kernel,
        out_shape=jax.ShapeDtypeStruct((width, width), BF16),
        grid=(1,),
        in_specs=[
            pl.BlockSpec((rows, bond), lambda i: (0, 0)),
            pl.BlockSpec((bond, width), lambda i: (0, 0)),
        ],
        out_specs=pl.BlockSpec((width, width), lambda i: (0, 0)),
        compiler_params=LARGE,
        cost_estimate=pl.CostEstimate(
            flops=2 * rows * bond * width,
            bytes_accessed=2 * bond * (rows + width),
            transcendentals=0,
        ),
    )(edge_wide, own_map)
    proj_blocks = lax.all_gather(proj, "x", axis=0)

    other = dot(cross_all, own_map).astype(BF16).reshape(blocks, -1, width)
    own = swap(other, "x")
    chosen = join_rows(jnp.where(before, other, own), "zl")
    chosen = spread(chosen, "y")
    chosen, proj_blocks = lax.optimization_barrier((chosen, proj_blocks))
    chosen = spread(chosen, "core")

    shares = pl.pallas_call(
        partial_kernel,
        out_shape=jax.ShapeDtypeStruct((blocks, rows, width), BF16),
        in_specs=[SMEM] + [VMEM] * 4,
        out_specs=VMEM,
        compiler_params=PARAMS,
    )(here, vector, chosen, proj_blocks, own_map)
    shares = swap(shares, "x")
    dedge, sums = pl.pallas_call(
        edge_kernel,
        out_shape=(
            jax.ShapeDtypeStruct((rows, width), F32),
            jax.ShapeDtypeStruct((8, 128), F32),
        ),
        in_specs=[VMEM, VMEM],
        out_specs=(VMEM, VMEM),
        compiler_params=PARAMS,
    )(vector, shares)
    sums = total(spread(sums, ("y", "core", "x")))
    sums = spread(sums, ("zh", "zl"))
    return pl.pallas_call(
        functools.partial(finish_kernel, float(rows_total * bond)),
        out_shape=(
            jax.ShapeDtypeStruct((rows, width), F32),
            jax.ShapeDtypeStruct((2,), F32),
        ),
        in_specs=[VMEM] * 3,
        out_specs=(VMEM, SMEM),
        compiler_params=PARAMS,
    )(sums, vector, dedge)


def solution(mesh):
    fine = Mesh(mesh.devices.reshape(4, 4, -1, 2, mesh.shape["col"]), ROW + ("x",))
    in_specs = (P(ROW, "x"), P(None, "x"), P(None, "x"), P(ROW, "x"))
    out_specs = (P(ROW, "x"), P())
    return jax.shard_map(
        on_device, mesh=fine, in_specs=in_specs, out_specs=out_specs, check_vma=False
    )
```

```python
import functools

import jax
import jax.numpy as jnp
from jax import lax
from jax.experimental import pallas as pl
from jax.experimental.pallas import tpu as pltpu
from jax.sharding import Mesh, PartitionSpec as P

BF16 = jnp.bfloat16
F32 = jnp.float32
ROW = ("y", "zh", "zl", "core")
VMEM = pl.BlockSpec(memory_space=pltpu.VMEM)
SMEM = pl.BlockSpec(memory_space=pltpu.SMEM)
PARAMS = pltpu.CompilerParams(vmem_limit_bytes=10 * 1024 * 1024)


def swap(pieces, axis):
    return lax.all_to_all(pieces, axis, split_axis=0, concat_axis=0, tiled=True)


def spread(block, axis):
    members = lax.axis_size(axis)
    return swap(jnp.broadcast_to(block[None], (members, *block.shape)), axis)


def total(pieces):
    return jnp.sum(pieces.astype(F32), axis=0)


def scatter_sum(block, axis):
    members = lax.axis_size(axis)
    pieces = block.reshape(members, block.shape[0] // members, block.shape[1])
    return total(swap(pieces, axis))


def join_rows(blocks, axis):
    stacked = spread(blocks, axis)
    members, count, rows, width = stacked.shape
    return stacked.transpose(1, 0, 2, 3).reshape(count, members * rows, width)


def dot(a, b):
    return jnp.dot(a, b, preferred_element_type=F32)


def dot_turned(a, b):
    return lax.dot_general(a, b, (((1,), (1,)), ((), ())), preferred_element_type=F32)


def add_kernel(pieces, out):
    out[...] = sum(pieces[i].astype(F32) for i in range(pieces.shape[0])).astype(BF16)


def proj_kernel(edge, own_map, out):
    rows = edge.shape[0]
    out[:rows] = dot(edge[...], own_map[...]).astype(BF16)
    out[rows:] = jnp.zeros((out.shape[0] - rows, out.shape[1]), BF16)


def partial_kernel(place, vec, sym, proj, own_map, out):
    rows, width = vec.shape
    blocks = proj.shape[0]
    first = lax.broadcasted_iota(jnp.int32, (width, width), 0)
    second = lax.broadcasted_iota(jnp.int32, (width, width), 1)
    zero = jnp.zeros((width, width), BF16)
    acc = jnp.zeros((rows, width), F32)
    for k in range(blocks):
        shift = (place[0] - k) * width
        block = jnp.concatenate(
            [sym[c, y, k] for c in range(sym.shape[0]) for y in range(sym.shape[1])]
        )
        part = proj[k, :rows]
        acc += dot(part, jnp.where(first <= second + shift, block, zero))
        acc += dot_turned(part, jnp.where(first < second - shift, block, zero))
    corrected = (vec[...] - acc).astype(BF16)
    for k in range(blocks):
        share = dot_turned(corrected, own_map[k * width : (k + 1) * width])
        out[k] = share.astype(BF16)


def fold(values):
    line = jnp.sum(values, axis=0, keepdims=True)
    return sum(line[:, i : i + 128] for i in range(0, values.shape[1], 128))


def edge_kernel(vec, shares, dedge, sums):
    acc = sum(shares[k].astype(F32) for k in range(shares.shape[0]))
    v = vec[...]
    dedge[...] = acc
    sums[...] = jnp.concatenate(
        [fold(v * v), fold(v * acc), fold(acc * acc), jnp.zeros((5, 128), F32)], axis=0
    )


def finish_kernel(count, sums, vec, dedge, out, coeffs):
    lines = sum(sums[i] for i in range(sums.shape[0]))
    vv, vd, dd = (jnp.sum(lines[i : i + 1], axis=1, keepdims=True) for i in range(3))
    along = (vv - vd) / count
    keep = 1.0 - along
    square = (keep * keep * vv - 2.0 * keep * vd + dd) / count
    scale = jnp.sqrt(jnp.maximum(square, 0.0) + 1e-06)
    inverse = 1.0 / scale
    out[...] = (keep * vec[...] - dedge[...]) * inverse
    coeffs[0] = along[0, 0]
    coeffs[1] = scale[0, 0]


def on_device(edge, corner, tri_inv, vector):
    bond, width = corner.shape
    rows = vector.shape[0]
    blocks = bond // width
    place = lax.axis_index("x")
    here = place[None]
    rows_total = rows * lax.axis_size(ROW)

    before = lax.broadcasted_iota(jnp.int32, (blocks, 1, 1), 0) < place
    edge, here, before = lax.optimization_barrier((edge, here, before))
    corner_wide = lax.all_gather(corner, "x", axis=1, tiled=True)
    edge_wide = lax.all_gather(edge, "x", axis=1, tiled=True)
    vec_low = vector.astype(BF16)
    cross = lax.dot_general(
        vec_low, edge_wide, (((0,), (0,)), ((), ())), preferred_element_type=F32
    )
    cross = cross * (1.0 / rows_total)
    pair = swap(cross.astype(BF16).reshape(2, -1, bond), "core")
    cross = pl.pallas_call(
        add_kernel,
        out_shape=jax.ShapeDtypeStruct(pair.shape[1:], BF16),
        in_specs=[VMEM],
        out_specs=VMEM,
        compiler_params=PARAMS,
    )(pair)
    for axis in ("y", "zl"):
        cross = scatter_sum(cross.astype(BF16), axis)
    cross = total(spread(cross.astype(BF16), "zh")).astype(BF16)
    cross_all = spread(cross, "x").reshape(-1, bond)

    own_map = dot(corner_wide, tri_inv).astype(BF16)
    proj = pl.pallas_call(
        proj_kernel,
        out_shape=jax.ShapeDtypeStruct((width, width), BF16),
        in_specs=[VMEM, VMEM],
        out_specs=VMEM,
        compiler_params=PARAMS,
        cost_estimate=pl.CostEstimate(
            flops=2 * rows * bond * width,
            bytes_accessed=2 * bond * (rows + width),
            transcendentals=0,
        ),
    )(edge_wide, own_map)
    proj_blocks = lax.all_gather(proj, "x", axis=0)

    other = dot(cross_all, own_map).astype(BF16).reshape(blocks, -1, width)
    own = swap(other, "x")
    chosen = join_rows(jnp.where(before, other, own), "zl")
    chosen = spread(chosen, "y")
    chosen, proj_blocks = lax.optimization_barrier((chosen, proj_blocks))
    chosen = spread(chosen, "core")

    shares = pl.pallas_call(
        partial_kernel,
        out_shape=jax.ShapeDtypeStruct((blocks, rows, width), BF16),
        in_specs=[SMEM] + [VMEM] * 4,
        out_specs=VMEM,
        compiler_params=PARAMS,
    )(here, vector, chosen, proj_blocks, own_map)
    shares = swap(shares, "x")
    dedge, sums = pl.pallas_call(
        edge_kernel,
        out_shape=(
            jax.ShapeDtypeStruct((rows, width), F32),
            jax.ShapeDtypeStruct((8, 128), F32),
        ),
        in_specs=[VMEM, VMEM],
        out_specs=(VMEM, VMEM),
        compiler_params=PARAMS,
    )(vector, shares)
    sums = total(spread(sums, ("zh", "zl")))
    sums = spread(sums, ("y", "core", "x"))
    return pl.pallas_call(
        functools.partial(finish_kernel, float(rows_total * bond)),
        out_shape=(
            jax.ShapeDtypeStruct((rows, width), F32),
            jax.ShapeDtypeStruct((2,), F32),
        ),
        in_specs=[VMEM] * 3,
        out_specs=(VMEM, SMEM),
        compiler_params=PARAMS,
    )(sums, vector, dedge)


def solution(mesh):
    fine = Mesh(mesh.devices.reshape(4, 4, -1, 2, mesh.shape["col"]), ROW + ("x",))
    in_specs = (P(ROW, "x"), P(None, "x"), P(None, "x"), P(ROW, "x"))
    out_specs = (P(ROW, "x"), P())
    return jax.shard_map(
        on_device, mesh=fine, in_specs=in_specs, out_specs=out_specs, check_vma=False
    )
```
